32 devices in a mesh: grp: 8 (over z, y), blk: 4 (over x, core).
Axes of the slice: x: 2, y: 2, z: 4, core: 2. Of those that a mesh axis runs over, the one named last changes fastest.
Arguments:
- images: bfloat16 [16, 1024, 1152], P('grp', 'blk'), may hold values from -6 to 6
- cotangent: bfloat16 [16, 1024, 1152], P('grp', 'blk'), may hold values from -6 to 6
- timestep: int32 [16], P('grp'), may hold values from 0 to 999
- input_weight: bfloat16 [1152, 3456], P('blk'), may hold values from -0.1875 to 0.1875
- input_bias: float32 [2304], replicated, may hold values from -3 to 3
- output_weight: bfloat16 [1152, 1152], P('blk'), may hold values from -0.75 to 0.75
- output_bias: float32 [1152], replicated, may hold values from -3 to 3
- expand_weight: bfloat16 [1152, 4608], P('blk'), may hold values from -0.1875 to 0.1875
- expand_bias: float32 [4608], replicated, may hold values from -3 to 3
- shrink_weight: bfloat16 [4608, 1152], P('blk'), may hold values from -0.09375 to 0.09375
- shrink_bias: float32 [1152], replicated, may hold values from -3 to 3
- modulate_weight: bfloat16 [1152, 6912], P('blk'), may hold values from -0.1875 to 0.1875
- modulate_bias: float32 [6912], replicated, may hold values from -4 to 4
- position_table: float32 [3969, 16], replicated, may hold values from -4 to 4
Outputs:
- result: bfloat16 [16, 1024, 1152], P('grp', 'blk')
- grad_images: bfloat16 [16, 1024, 1152], P('grp', 'blk')
- grad_input_weight: float32 [1152, 3456], P('blk')
- grad_input_bias: float32 [2304], P('blk')
- grad_output_weight: float32 [1152, 1152], P('blk')
- grad_output_bias: float32 [1152], P('blk')
- grad_expand_weight: float32 [1152, 4608], P('blk')
- grad_expand_bias: float32 [4608], P('blk')
- grad_shrink_weight: float32 [4608, 1152], P('blk')
- grad_shrink_bias: float32 [1152], P('blk')
- grad_modulate_weight: float32 [1152, 6912], P('blk')
- grad_modulate_bias: float32 [6912], P('blk')
- grad_position_table: float32 [3969, 16], replicated
The draws below stay inside these ranges and needn't reach their ends.
All inputs are finite; a program needn't handle non-finite values.
Results may differ from the reference program's by a relative error of at most 0.023.
Values may be sent and summed in bfloat16 or wider, within the bound.
No kernel may reach another device: no remote copies, remote signals or barrier semaphores. Data moves between devices by JAX's collectives and lax.ppermute only.
A program may use at most 384 MiB of HBM per device.

```python
import math
import jax
import jax.numpy as jnp
from jax import lax

D = 1152
HEADS = 16
HD = 72
FF = 4608
GRID = 32
NSTEPS = 1000
SEQ = 1024
IMAGES = 16
TABLE = 3969


def plant(entries, stream_key, smallest, largest):
    longest = entries.shape.index(max(entries.shape))
    spots = []
    for shift in (0, 1):
        where = [jax.random.randint(jax.random.fold_in(stream_key, axis), (), 0, length) for axis, length in enumerate(entries.shape)]
        where[longest] = (where[longest] + shift) % entries.shape[longest]
        spots.append(tuple(where))
    return entries.at[spots[0]].set(smallest).at[spots[1]].set(largest)


def level_of(stream_key, extent, cuts, least, top_value):
    factor_of, own = 1.0, jax.random.fold_in(stream_key, 6)
    for position, parts in cuts:
        draws = jnp.exp(jax.random.uniform(jax.random.fold_in(own, position), (parts,), jnp.float32, least / len(cuts), top_value / len(cuts)))
        factor_of = factor_of * jnp.repeat(draws, extent[position] // parts).reshape([-1 if axis == position else 1 for axis in range(len(extent))])
    return factor_of


def bell_draw(stream_key, extent, spread, reach, shards=(), held_as=jnp.bfloat16):
    gain = level_of(stream_key, extent, shards, -0.22, 0.18) if shards else 1.0
    entries = jax.random.normal(stream_key, extent, jnp.float32) * spread * gain
    return jnp.minimum(jnp.maximum(entries, -reach), reach).astype(held_as)


def setup_inputs(seed: int = 0) -> dict:
    splits = jax.random.split(jax.random.key(seed), 15)
    images = bell_draw(splits[0], (IMAGES, SEQ, D), 1.0, 6.0, ((0, 8), (1, 4)))
    cotangent = bell_draw(splits[1], (IMAGES, SEQ, D), 1.0, 6.0, ((0, 8), (1, 4)))
    timestep = plant(jax.random.randint(splits[2], (IMAGES,), 0, NSTEPS), jax.random.fold_in(splits[2], 1), 0, NSTEPS - 1).astype(jnp.int32)
    input_weight = bell_draw(splits[3], (D, 3 * D), D ** -0.5, 0.1875, ((0, 4),))
    input_bias = bell_draw(splits[4], (2 * D,), 0.5, 3.0, (), jnp.float32)
    output_weight = bell_draw(splits[5], (D, D), (D // 16) ** -0.5, 0.75, ((0, 4),))
    output_bias = bell_draw(splits[6], (D,), 0.5, 3.0, (), jnp.float32)
    expand_weight = bell_draw(splits[7], (D, FF), D ** -0.5, 0.1875, ((0, 4),))
    expand_bias = bell_draw(splits[8], (FF,), 0.5, 3.0, (), jnp.float32)
    shrink_weight = bell_draw(splits[9], (FF, D), FF ** -0.5, 0.09375, ((0, 4),))
    shrink_bias = bell_draw(splits[10], (D,), 0.5, 3.0, (), jnp.float32)
    modulate_weight = bell_draw(splits[11], (D, 6 * D), D ** -0.5, 0.1875, ((0, 4),))
    modulate_bias = bell_draw(splits[12], (6 * D,), 1.0, 4.0, (), jnp.float32)
    position_table = bell_draw(splits[13], (TABLE, HEADS), 1.0, 4.0, (), jnp.float32)
    return dict(images=images, cotangent=cotangent, timestep=timestep, input_weight=input_weight, input_bias=input_bias, output_weight=output_weight, output_bias=output_bias, expand_weight=expand_weight, expand_bias=expand_bias, shrink_weight=shrink_weight, shrink_bias=shrink_bias, modulate_weight=modulate_weight, modulate_bias=modulate_bias, position_table=position_table)


HIGHEST = lax.Precision.HIGHEST

@jax.custom_vjp
def low(v):
    return lax.optimization_barrier(v.astype(jnp.bfloat16)).astype(jnp.float32)

@jax.custom_vjp
def low_back(v):
    return v

def low_keep(v):
    return (low(v), None)

def low_pass(kept, grad):
    return (grad,)

def back_keep(v):
    return (v, None)

def back_low(kept, grad):
    return (low(grad),)
low.defvjp(low_keep, low_pass)
low_back.defvjp(back_keep, back_low)

def narrow(value):
    return low(low_back(value))

def embedding(step_values, width):
    half_width = width // 2
    frequency = jnp.exp(-math.log(10000.0) * jnp.arange(half_width, dtype=jnp.float32) / half_width)
    angles = step_values.astype(jnp.float32)[:, None] * frequency[None, :]
    return jnp.concatenate([jnp.cos(angles), jnp.sin(angles)], axis=-1)

def norm_rows(values):
    centered = values - lax.optimization_barrier(jnp.mean(values, axis=-1, keepdims=True))
    variance = lax.optimization_barrier(jnp.mean(centered * centered, axis=-1, keepdims=True))
    return centered * lax.rsqrt(variance + 1e-06)

def pair_index():
    places = jnp.arange(SEQ, dtype=jnp.int32)
    rows_of = places // GRID
    cols_of = places % GRID
    return ((rows_of[:, None] - rows_of[None, :] + GRID - 1) * (2 * GRID - 1) + cols_of[:, None] - cols_of[None, :] + GRID - 1).astype(jnp.int32)

def one_image(weights, tokens, modulation_row, index_table):
    input_weight, input_bias, output_weight, output_bias, expand_weight, expand_bias, shrink_weight, shrink_bias, position_table = weights
    shift_one, scale_one, gate_one, shift_two, scale_two, gate_two = jnp.split(modulation_row, 6)
    hidden_one = low(norm_rows(tokens) * (1.0 + scale_one) + shift_one)
    projected = jnp.dot(hidden_one, input_weight, precision=HIGHEST)
    queries = narrow(projected[:, :D] + input_bias[:D]).reshape(SEQ, HEADS, HD)
    keys_all = narrow(projected[:, D:2 * D]).reshape(SEQ, HEADS, HD)
    values_all = narrow(projected[:, 2 * D:] + input_bias[D:]).reshape(SEQ, HEADS, HD)
    bias_heads = jnp.transpose(position_table[index_table], (2, 0, 1))
    scores = jnp.einsum('qhd,khd->hqk', queries, keys_all, precision=HIGHEST) * HD ** (-0.5) + bias_heads
    scores = low_back(scores)
    softmax_weights = jax.nn.softmax(scores, axis=-1)
    attended = jnp.einsum('hqk,khd->qhd', low(softmax_weights), values_all, precision=HIGHEST)
    attended = narrow(attended.reshape(SEQ, D))
    branch_one = low_back(jnp.dot(attended, output_weight, precision=HIGHEST) + output_bias)
    middle = tokens + gate_one * branch_one
    hidden_two = low(norm_rows(middle) * (1.0 + scale_two) + shift_two)
    expanded = low_back(jnp.dot(hidden_two, expand_weight, precision=HIGHEST) + expand_bias)
    activated = low(jax.nn.gelu(expanded, approximate=True))
    branch_two = low_back(jnp.dot(activated, shrink_weight, precision=HIGHEST) + shrink_bias)
    return middle + gate_two * branch_two

def forward(weights, modulate_weight, modulate_bias, images, condition):
    modulation = jnp.dot(condition, modulate_weight, precision=HIGHEST) + modulate_bias
    index_table = pair_index()

    def per_image(items):
        return one_image(weights, items[0], items[1], index_table)
    return lax.map(jax.checkpoint(per_image), (images, modulation))

def reference(images, cotangent, timestep, input_weight, input_bias, output_weight, output_bias, expand_weight, expand_bias, shrink_weight, shrink_bias, modulate_weight, modulate_bias, position_table):
    weights = tuple((member.astype(jnp.float32) for member in (input_weight, input_bias, output_weight, output_bias, expand_weight, expand_bias, shrink_weight, shrink_bias, position_table)))
    condition = low(jax.nn.silu(embedding(timestep, D)))

    def with_condition(weight_set, mod_weight, mod_bias, image_values):
        return forward(weight_set, mod_weight, mod_bias, image_values, condition)
    output_values, pullback = jax.vjp(with_condition, weights, modulate_weight.astype(jnp.float32), modulate_bias.astype(jnp.float32), images.astype(jnp.float32))
    weight_grads, mod_weight_grad, mod_bias_grad, image_grad = pullback(cotangent.astype(jnp.float32))
    return (output_values.astype(jnp.bfloat16), image_grad.astype(jnp.bfloat16), weight_grads[0], weight_grads[1], weight_grads[2], weight_grads[3], weight_grads[4], weight_grads[5], weight_grads[6], weight_grads[7], mod_weight_grad, mod_bias_grad, weight_grads[8])
```

```python
import functools
import math

import jax
import jax.numpy as jnp
from jax import lax
from jax.experimental import pallas as pl
from jax.experimental.pallas import tpu as pltpu
from jax.sharding import PartitionSpec as P

GRID = 32
F32 = jnp.float32
LOW = jnp.bfloat16
HIGHEST = lax.Precision.HIGHEST
TILE = 256
LANES = 128
MIB = 2**20


def dot(left, right, left_dim, right_dim):
    return lax.dot_general(
        left, right, (((left_dim,), (right_dim,)), ((), ())), preferred_element_type=F32
    )


def call(kernel, grid, in_specs, out_specs, out_shape, scratch=(), mib=56):
    return pl.pallas_call(
        kernel,
        grid=grid,
        in_specs=in_specs,
        out_specs=out_specs,
        out_shape=out_shape,
        scratch_shapes=list(scratch),
        compiler_params=pltpu.CompilerParams(vmem_limit_bytes=mib * MIB),
    )


def shape(dims, kind=F32):
    return jax.ShapeDtypeStruct(dims, kind)


def whole(dims):
    return pl.BlockSpec(dims, lambda *_: (0,) * len(dims))


def norm_rows(values):
    centered = values - jnp.mean(values, axis=-1, keepdims=True)
    variance = jnp.mean(centered * centered, axis=-1, keepdims=True)
    inverse = lax.rsqrt(variance + 1e-06)
    return centered * inverse, inverse


def norm_back(grad_normed, normed, inverse):
    first = jnp.mean(grad_normed, axis=-1, keepdims=True)
    second = jnp.mean(grad_normed * normed, axis=-1, keepdims=True)
    return inverse * (grad_normed - first - normed * second)


def project_kernel(parts, head_dim, x_ref, mod_ref, w_ref, b_ref, h_ref, o_ref):
    normed, _ = norm_rows(x_ref[...].astype(F32))
    hidden = (normed * (1.0 + mod_ref[1:2]) + mod_ref[0:1]).astype(LOW)
    h_ref[...] = hidden
    low = (dot(hidden, w_ref[...], 1, 0) + b_ref[...]).astype(LOW)
    for part in range(parts):
        o_ref[part] = low[:, part * head_dim : (part + 1) * head_dim]


def project(tokens, mod, weight, bias, head_dim):
    count, width = tokens.shape
    columns = weight.shape[1]
    parts = columns // head_dim
    return call(
        functools.partial(project_kernel, parts, head_dim),
        (count // TILE,),
        [
            pl.BlockSpec((TILE, width), lambda i: (i, 0)),
            whole(mod.shape),
            whole(weight.shape),
            whole((1, columns)),
        ],
        [
            pl.BlockSpec((TILE, width), lambda i: (i, 0)),
            pl.BlockSpec((parts, TILE, head_dim), lambda i: (0, i, 0)),
        ],
        [shape((count, width), LOW), shape((parts, count, head_dim), LOW)],
    )(tokens, mod, weight, bias)


def bias_tile(table_ref, head, tile, keys):
    pieces = []
    per = TILE // LANES
    last = keys // LANES - 1
    for piece in range(per):
        start = (last - (tile * per + piece)) * LANES
        pieces.append(table_ref[head, start : start + keys, :])
    return jnp.concatenate(pieces, axis=1)


def attend_kernel(q_ref, k_ref, v_ref, table_ref, o_ref, lse_ref):
    heads, count, head_dim = q_ref.shape
    scale = head_dim ** (-0.5)
    for tile in range(count // TILE):
        outs, logs = [], []
        for head in range(heads):
            span = slice(tile * TILE, (tile + 1) * TILE)
            scores = dot(k_ref[head], q_ref[head, span, :], 1, 1) * scale
            scores = scores + bias_tile(table_ref, head, tile, k_ref.shape[1])
            largest = jnp.max(scores, axis=0, keepdims=True)
            exponent = jnp.exp(scores - largest)
            total = jnp.sum(exponent, axis=0, keepdims=True)
            out = dot(v_ref[head], exponent.astype(LOW), 0, 0)
            outs.append(out / total)
            logs.append(largest + jnp.log(total))
        o_ref[:, span] = jnp.concatenate(outs, axis=0).astype(LOW)
        lse_ref[0, :, span] = jnp.concatenate(logs, axis=0)


def attend(parts, table, heads, pair):
    _, count, head_dim = parts.shape
    groups = heads // pair

    def head_block(first):
        return pl.BlockSpec(
            (pair, count, head_dim), lambda i, first=first: (first * groups + i, 0, 0)
        )

    return call(
        attend_kernel,
        (groups,),
        [
            head_block(0),
            head_block(1),
            head_block(2),
            pl.BlockSpec((pair,) + table.shape[1:], lambda i: (i, 0, 0)),
        ],
        [
            pl.BlockSpec((pair * head_dim, count), lambda i: (i, 0)),
            pl.BlockSpec((1, pair, count), lambda i: (i, 0, 0)),
        ],
        [shape((heads * head_dim, count), LOW), shape((groups, pair, count))],
    )(parts, parts, parts, table)


def attend_back_kernel(
    q_ref, k_ref, v_ref, go_ref, o_ref, lse_ref, table_ref, gq_ref, gk_ref, gv_ref, gt_ref
):
    heads, count, head_dim = q_ref.shape
    keys = k_ref.shape[1]
    scale = head_dim ** (-0.5)
    per = TILE // LANES
    last = keys // LANES - 1
    gt_ref[...] = jnp.zeros_like(gt_ref)
    for head in range(heads):
        key = k_ref[head]
        value = v_ref[head]
        grad_key = jnp.zeros((keys, head_dim), F32)
        grad_value = jnp.zeros((keys, head_dim), F32)
        for tile in range(count // TILE):
            span = slice(tile * TILE, (tile + 1) * TILE)
            query = q_ref[head, span, :]
            grad_out = go_ref[head, span, :]
            scores = dot(key, query, 1, 1) * scale + bias_tile(table_ref, head, tile, keys)
            probs = jnp.exp(scores - lse_ref[0, head : head + 1, span])
            grad_probs = dot(value, grad_out, 1, 1)
            out = o_ref[head * head_dim : (head + 1) * head_dim, span].astype(F32)
            row_dot = jnp.sum(out * grad_out.astype(F32).T, axis=0, keepdims=True)
            grad_scores = probs * (grad_probs - row_dot)
            for piece in range(per):
                start = (last - (tile * per + piece)) * LANES
                gt_ref[head, start : start + keys, :] += grad_scores[
                    :, piece * LANES : (piece + 1) * LANES
                ]
            low = grad_scores.astype(LOW)
            grad_value = grad_value + dot(probs.astype(LOW), grad_out, 1, 0)
            grad_key = grad_key + dot(low, query, 1, 0)
            gq_ref[head, span, :] = (dot(key, low, 0, 0) * scale).T.astype(LOW)
        gk_ref[head] = (grad_key * scale).astype(LOW)
        gv_ref[head] = grad_value.astype(LOW)


def attend_back(parts, grad_out, attended, log_total, table, heads, pair):
    _, count, head_dim = parts.shape
    groups = heads // pair

    def head_block(first):
        return pl.BlockSpec(
            (pair, count, head_dim), lambda i, first=first: (first * groups + i, 0, 0)
        )

    table_block = pl.BlockSpec((pair,) + table.shape[1:], lambda i: (i, 0, 0))
    return call(
        attend_back_kernel,
        (groups,),
        [
            head_block(0),
            head_block(1),
            head_block(2),
            head_block(0),
            pl.BlockSpec((pair * head_dim, count), lambda i: (i, 0)),
            pl.BlockSpec((1, pair, count), lambda i: (i, 0, 0)),
            table_block,
        ],
        [head_block(0)] * 3 + [table_block],
        [shape((heads, count, head_dim), LOW)] * 3 + [shape(table.shape)],
    )(parts, parts, parts, grad_out, attended, log_total, table)


def middle_kernel(
    att_ref, w_ref, ob_ref, x_ref, cot_ref, mod_ref, br_ref, mid_ref, h_ref, gb_ref, sum_ref
):
    branch = dot(att_ref[...], w_ref[...], 0, 0) + ob_ref[...]
    middle = x_ref[...].astype(F32) + mod_ref[2:3] * branch
    normed, _ = norm_rows(middle)
    br_ref[...] = branch.astype(LOW)
    mid_ref[...] = middle
    h_ref[...] = (normed * (1.0 + mod_ref[4:5]) + mod_ref[3:4]).astype(LOW)
    grad = (mod_ref[5:6] * cot_ref[...].astype(F32)).astype(LOW)
    gb_ref[...] = grad

    @pl.when(pl.program_id(0) == 0)
    def _():
        sum_ref[...] = jnp.zeros_like(sum_ref)

    sum_ref[...] += jnp.sum(grad.astype(F32), axis=0, keepdims=True)


def middle_part(attended, weight, bias, tokens, cotangent, mod):
    count, width = tokens.shape
    rows = pl.BlockSpec((TILE, width), lambda i: (i, 0))
    return call(
        middle_kernel,
        (count // TILE,),
        [
            pl.BlockSpec((attended.shape[0], TILE), lambda i: (0, i)),
            whole(weight.shape),
            whole((1, width)),
            rows,
            rows,
            whole(mod.shape),
        ],
        [rows, rows, rows, rows, whole((1, width))],
        [
            shape((count, width), LOW),
            shape((count, width)),
            shape((count, width), LOW),
            shape((count, width), LOW),
            shape((1, width)),
        ],
    )(attended, weight, bias, tokens, cotangent, mod)


def feed_kernel(
    h_ref, g_ref, we_ref, ws_ref, be_ref, act_ref, ge_ref, sum_ref, b2_ref, gh_ref, b2_acc, gh_acc
):
    step = pl.program_id(0)
    hidden, grad, expand, shrink = h_ref[...], g_ref[...], we_ref[...], ws_ref[...]
    inner = dot(hidden, expand, 1, 0) + be_ref[...]
    slope = math.sqrt(2.0 / math.pi)
    square = inner * inner
    bent = jnp.tanh(slope * (inner + 0.044715 * inner * square))
    act = (0.5 * inner * (1.0 + bent)).astype(LOW)
    act_ref[...] = act
    back = 0.5 * (1.0 + bent) + 0.5 * inner * (1.0 - bent * bent) * (
        slope * (1.0 + 3 * 0.044715 * square)
    )
    grad_inner = (dot(grad, shrink, 1, 1) * back).astype(LOW)
    ge_ref[...] = grad_inner
    sum_ref[...] = jnp.sum(grad_inner.astype(F32), axis=0, keepdims=True)

    @pl.when(step == 0)
    def _():
        b2_acc[...] = dot(act, shrink, 1, 0)
        gh_acc[...] = dot(grad_inner, expand, 1, 1)

    @pl.when(step > 0)
    def _():
        b2_acc[...] += dot(act, shrink, 1, 0)
        gh_acc[...] += dot(grad_inner, expand, 1, 1)

    @pl.when(step == pl.num_programs(0) - 1)
    def _():
        b2_ref[...] = b2_acc[...].astype(LOW)
        gh_ref[...] = gh_acc[...].astype(LOW)


def feed(hidden, grad, expand, shrink, bias, chunk):
    count, width = hidden.shape
    inner = expand.shape[1]
    return call(
        feed_kernel,
        (inner // chunk,),
        [
            whole(hidden.shape),
            whole(grad.shape),
            pl.BlockSpec((width, chunk), lambda i: (0, i)),
            pl.BlockSpec((chunk, width), lambda i: (i, 0)),
            pl.BlockSpec((1, chunk), lambda i: (0, i)),
        ],
        [
            pl.BlockSpec((count, chunk), lambda i: (0, i)),
            pl.BlockSpec((count, chunk), lambda i: (0, i)),
            pl.BlockSpec((1, chunk), lambda i: (0, i)),
            whole((count, width)),
            whole((count, width)),
        ],
        [
            shape((count, inner), LOW),
            shape((count, inner), LOW),
            shape((1, inner)),
            shape((count, width), LOW),
            shape((count, width), LOW),
        ],
        [pltpu.VMEM((count, width), F32)] * 2,
    )(hidden, grad, expand, shrink, bias)


def branch_back_kernel(
    head_dim,
    own_ref,
    got_ref,
    mid_ref,
    cot_ref,
    br_ref,
    w_ref,
    mod_ref,
    gm_ref,
    gb_ref,
    ga_ref,
    sum_ref,
):
    grad_hidden = own_ref[...].astype(F32) + got_ref[...].astype(F32)
    normed, inverse = norm_rows(mid_ref[...])
    grad_middle = cot_ref[...].astype(F32) + norm_back(
        grad_hidden * (1.0 + mod_ref[4:5]), normed, inverse
    )
    gm_ref[...] = grad_middle
    grad_branch = (mod_ref[2:3] * grad_middle).astype(LOW)
    gb_ref[...] = grad_branch
    grad_att = dot(grad_branch, w_ref[...], 1, 1).astype(LOW)
    for part in range(ga_ref.shape[0]):
        ga_ref[part] = grad_att[:, part * head_dim : (part + 1) * head_dim]

    @pl.when(pl.program_id(0) == 0)
    def _():
        sum_ref[...] = jnp.zeros_like(sum_ref)

    sum_ref[0:1] += jnp.sum(grad_hidden, axis=0, keepdims=True)
    sum_ref[1:2] += jnp.sum(grad_hidden * normed, axis=0, keepdims=True)
    sum_ref[2:3] += jnp.sum(grad_middle * br_ref[...].astype(F32), axis=0, keepdims=True)
    sum_ref[3:4] += jnp.sum(grad_branch.astype(F32), axis=0, keepdims=True)


def branch_back(own, got, middle, cotangent, branch, weight, mod, head_dim):
    count, width = own.shape
    rows = pl.BlockSpec((TILE, width), lambda i: (i, 0))
    parts = weight.shape[0] // head_dim
    return call(
        functools.partial(branch_back_kernel, head_dim),
        (count // TILE,),
        [rows, rows, rows, rows, rows, whole(weight.shape), whole(mod.shape)],
        [
            rows,
            rows,
            pl.BlockSpec((parts, TILE, head_dim), lambda i: (0, i, 0)),
            whole((8, width)),
        ],
        [
            shape((count, width)),
            shape((count, width), LOW),
            shape((parts, count, head_dim), LOW),
            shape((8, width)),
        ],
    )(own, got, middle, cotangent, branch, weight, mod)


def project_back_kernel(gq_ref, gk_ref, gv_ref, w_ref, x_ref, g_ref, gh_ref, sum_ref, bias_ref):
    pieces = [ref[part] for ref in (gq_ref, gk_ref, gv_ref) for part in range(ref.shape[0])]
    joined = jnp.concatenate(pieces, axis=1)
    g_ref[...] = joined
    grad_hidden = dot(joined, w_ref[...], 1, 1)
    gh_ref[...] = grad_hidden.astype(LOW)
    normed, _ = norm_rows(x_ref[...].astype(F32))

    @pl.when(pl.program_id(0) == 0)
    def _():
        sum_ref[...] = jnp.zeros_like(sum_ref)
        bias_ref[...] = jnp.zeros_like(bias_ref)

    sum_ref[0:1] += jnp.sum(grad_hidden, axis=0, keepdims=True)
    sum_ref[1:2] += jnp.sum(grad_hidden * normed, axis=0, keepdims=True)
    bias_ref[...] += jnp.sum(joined.astype(F32), axis=0, keepdims=True)


def project_back(grad_query, grad_key, grad_value, weight, tokens):
    count, width = tokens.shape
    columns = weight.shape[1]
    heads, _, head_dim = grad_query.shape
    rows = pl.BlockSpec((TILE, width), lambda i: (i, 0))
    part = pl.BlockSpec((heads, TILE, head_dim), lambda i: (0, i, 0))
    return call(
        project_back_kernel,
        (count // TILE,),
        [part, part, part, whole(weight.shape), rows],
        [
            pl.BlockSpec((TILE, columns), lambda i: (i, 0)),
            rows,
            whole((8, width)),
            whole((1, columns)),
        ],
        [
            shape((count, columns), LOW),
            shape((count, width), LOW),
            shape((8, width)),
            shape((1, columns)),
        ],
    )(grad_query, grad_key, grad_value, weight, tokens)


def input_back_kernel(own_ref, got_ref, x_ref, gm_ref, mod_ref, o_ref):
    grad_hidden = own_ref[...].astype(F32) + got_ref[...].astype(F32)
    normed, inverse = norm_rows(x_ref[...].astype(F32))
    grad = gm_ref[...] + norm_back(grad_hidden * (1.0 + mod_ref[1:2]), normed, inverse)
    o_ref[...] = grad.astype(LOW)


def input_back(own, got, tokens, grad_middle, mod):
    count, width = own.shape
    rows = pl.BlockSpec((TILE, width), lambda i: (i, 0))
    return call(
        input_back_kernel,
        (count // TILE,),
        [rows, rows, rows, rows, whole(mod.shape)],
        rows,
        shape((count, width), LOW),
    )(own, got, tokens, grad_middle, mod)


def swap_core(value):
    return lax.ppermute(value, "blk", [(i, i ^ 1) for i in range(4)])


def swap_chip(value):
    return lax.ppermute(value, "blk", [(i, i ^ 2) for i in range(4)])


def swap_group(value, bit):
    return lax.ppermute(value, "grp", [(i, i ^ bit) for i in range(lax.axis_size("grp"))])


def ordered(mine, other, place, axis=0):
    first = jnp.where(place == 0, mine, other)
    second = jnp.where(place == 0, other, mine)
    return jnp.concatenate([first, second], axis=axis)


def split_at(value, place, axis):
    half = value.shape[axis] // 2
    keep = lax.dynamic_slice_in_dim(value, place * half, half, axis)
    send = lax.dynamic_slice_in_dim(value, (1 - place) * half, half, axis)
    return keep, send


def add_low(one, two):
    return (one.astype(F32) + two.astype(F32)).astype(LOW)


def group_bits():
    count = lax.axis_size("grp")
    return [1 << i for i in range(count.bit_length() - 1)]


def bit_of(bit):
    return (lax.axis_index("grp") // bit) % 2


def scatter_groups(value, axis):
    for bit in group_bits():
        keep, send = split_at(value, bit_of(bit), axis)
        value = add_low(keep, swap_group(send, bit))
    return value


def gather_groups(value, axis):
    for bit in reversed(group_bits()):
        value = ordered(value, swap_group(value, bit), bit_of(bit), axis)
    return value


def table_picks(grid_side):
    span = 2 * grid_side - 1
    per = LANES // grid_side
    piece = jnp.arange(per, dtype=jnp.int32)
    offset = jnp.arange(span, dtype=jnp.int32)
    across = jnp.arange(grid_side, dtype=jnp.int32)
    same_piece = piece[:, None] == piece[None, :]
    same_offset = (
        across[None, None, :] - across[None, :, None] + grid_side - 1 == offset[:, None, None]
    )
    picks = same_piece[:, None, None, :, None] & same_offset[None, :, :, None, :]
    return picks.reshape(per * span, grid_side * LANES).astype(F32)


def table_rows(grid_side):
    return 2 * grid_side - LANES // grid_side


def spread_table(table, grid_side):
    span = 2 * grid_side - 1
    per = LANES // grid_side
    heads = table.shape[1]
    grid_table = table.T.reshape(heads, span, span)
    count = table_rows(grid_side)
    flipped = grid_table[:, ::-1]
    shifted = [
        flipped[:, per - 1 - piece : per - 1 - piece + count] for piece in range(per)
    ]
    stacked = jnp.stack(shifted, axis=2).reshape(heads * count, per * span)
    spread = jnp.dot(stacked, table_picks(grid_side), precision=HIGHEST)
    return spread.reshape(heads, count * grid_side, LANES)


def gather_table(grads, grid_side):
    span = 2 * grid_side - 1
    per = LANES // grid_side
    heads = grads.shape[0]
    count = table_rows(grid_side)
    flat = grads.reshape(heads * count, grid_side * LANES)
    picked = lax.dot_general(
        flat, table_picks(grid_side), (((1,), (1,)), ((), ())), precision=HIGHEST
    ).reshape(heads, count, per, span)
    total = sum(
        jnp.pad(
            picked[:, :, piece],
            ((0, 0), (per - 1 - piece, span - count - (per - 1 - piece)), (0, 0)),
        )
        for piece in range(per)
    )
    return total[:, ::-1].reshape(heads, span * span)


def embedding(step_values, width):
    half_width = width // 2
    frequency = jnp.exp(-math.log(10000.0) * jnp.arange(half_width, dtype=F32) / half_width)
    angles = step_values.astype(F32)[:, None] * frequency[None, :]
    return jnp.concatenate([jnp.cos(angles), jnp.sin(angles)], axis=-1)


def pick(value, place, axis=0):
    return lax.dynamic_index_in_dim(value, place, axis, keepdims=False)


def shards(
    images,
    cotangent,
    timestep,
    input_weight,
    input_bias,
    output_weight,
    output_bias,
    expand_weight,
    expand_bias,
    shrink_weight,
    shrink_bias,
    modulate_weight,
    modulate_bias,
    position_table,
):
    _, block_tokens, width = images.shape
    heads_all = position_table.shape[1]
    head_dim = width // heads_all
    heads = heads_all // 2
    feed_width = expand_weight.shape[1]
    own_rows = modulate_weight.shape[0]
    block = lax.axis_index("blk")
    chip, core = block // 2, block % 2

    condition = jax.nn.silu(embedding(timestep, width)).astype(LOW)
    condition_own = lax.dynamic_slice_in_dim(condition, block * own_rows, own_rows, 1)
    partial = jnp.dot(condition_own, modulate_weight, preferred_element_type=F32)
    partial = partial.reshape(2, -1, LANES)
    summed = pick(partial, core) + swap_core(pick(partial, 1 - core))
    summed = summed + swap_chip(summed)
    mod = (summed.reshape(-1) + modulate_bias).reshape(6, width)

    def gather_columns(weight, pieces):
        cut = weight.reshape(own_rows, pieces, 2, -1)
        mine = pick(cut, chip, 2).reshape(own_rows, -1)
        other = swap_chip(pick(cut, 1 - chip, 2).reshape(own_rows, -1))
        both = ordered(mine[None], other[None], chip)
        return ordered(both[:, None], swap_core(both)[:, None], core, 1).reshape(width, -1)

    def own_image(value):
        mine = pick(value, core)
        half = ordered(mine, swap_core(pick(value, 1 - core)), core)
        return half, ordered(half, swap_chip(half), chip)

    weight_in = gather_columns(input_weight, 3)
    tokens_half, tokens = own_image(images)
    cot_half, cot = own_image(cotangent)
    weight_out_pair = ordered(output_weight[None], swap_chip(output_weight)[None], chip)
    weight_out = ordered(
        weight_out_pair[:, None], swap_core(weight_out_pair)[:, None], core, 1
    ).reshape(width, width)
    weight_expand = gather_columns(expand_weight, 1)
    weight_shrink = ordered(shrink_weight, swap_core(shrink_weight), core)

    def own_half(vector):
        return lax.dynamic_slice_in_dim(vector, chip * (vector.shape[0] // 2), vector.shape[0] // 2, 0)

    bias_in = jnp.concatenate(
        [
            own_half(input_bias[:width]),
            jnp.zeros((width // 2,), F32),
            own_half(input_bias[width:]),
        ]
    )[None]
    table = spread_table(
        lax.dynamic_slice_in_dim(position_table, chip * heads, heads, 1), GRID
    )

    hidden_one, parts = project(tokens, mod, weight_in, bias_in, head_dim)
    attended, log_total = attend(parts, table, heads, 2)
    attended_all = ordered(attended, swap_chip(attended), chip)
    branch_one, middle, hidden_two, grad_branch_two, shrink_bias_grad = middle_part(
        attended_all, weight_out, output_bias[None], tokens, cot, mod
    )
    activated, grad_expanded, expand_bias_grad, branch_two, grad_hidden_two = feed(
        hidden_two, grad_branch_two, weight_expand, weight_shrink, own_half(expand_bias)[None], 384
    )
    half_count = tokens_half.shape[0]

    def half_of(value, place):
        return lax.dynamic_slice_in_dim(value, place * half_count, half_count, 0)

    grad_hidden_two_got = swap_chip(grad_hidden_two)
    branch_two_got = swap_chip(half_of(branch_two, 1 - chip))
    grad_middle, grad_branch_one, grad_attended, sums_two = branch_back(
        grad_hidden_two,
        grad_hidden_two_got,
        middle,
        cot,
        branch_one,
        lax.dynamic_slice_in_dim(weight_out, chip * (width // 2), width // 2, 0),
        mod,
        head_dim,
    )
    shrink_grad = dot(activated, grad_branch_two, 0, 0).astype(LOW)
    expand_grad = dot(hidden_two, grad_expanded, 0, 0).astype(LOW)
    output_grad = dot(attended, grad_branch_one, 1, 0).astype(LOW)
    grad_query, grad_key, grad_value, table_grad = attend_back(
        parts, grad_attended, attended, log_total, table, heads, 2
    )
    grad_projected, grad_hidden_one, sums_one, projected_bias_grad = project_back(
        grad_query, grad_key, grad_value, weight_in, tokens
    )
    grad_hidden_one_got = swap_chip(half_of(grad_hidden_one, 1 - chip))
    input_grad = dot(hidden_one, grad_projected, 0, 0).astype(LOW)
    grad_tokens = input_back(
        half_of(grad_hidden_one, chip),
        grad_hidden_one_got,
        tokens_half,
        half_of(grad_middle, chip),
        mod,
    )

    branch_two_half = (
        half_of(branch_two, chip).astype(F32) + branch_two_got.astype(F32) + shrink_bias
    )
    result_half = (half_of(middle, chip) + mod[5:6] * branch_two_half).astype(LOW)
    grad_gate_two = jnp.sum(cot_half.astype(F32) * branch_two_half, axis=0)

    def to_blocks(value):
        cut = value.reshape(2, block_tokens, width)
        mine = pick(cut, core)
        other = swap_core(pick(cut, 1 - core))
        return ordered(mine[None], other[None], core)

    result = to_blocks(result_half)
    grad_images = to_blocks(grad_tokens)

    def reduce_rows(grad):
        keep, send = split_at(grad, core, 0)
        return gather_groups(scatter_groups(add_low(keep, swap_core(send)), 0), 0).astype(F32)

    def reduce_columns(grad, pieces):
        keep, send = split_at(grad.reshape(2, 2, own_rows, -1), core, 1)
        cut = add_low(keep, swap_core(send)).reshape(2, own_rows, -1)
        cut = scatter_groups(cut, 1)
        mine = pick(cut, chip)
        other = swap_chip(pick(cut, 1 - chip))
        rows = mine.shape[0]
        mine, other = mine.reshape(rows, pieces, 1, -1), other.reshape(rows, pieces, 1, -1)
        joined = ordered(mine, other, chip, 2).reshape(rows, -1)
        return gather_groups(joined, 0).astype(F32)

    total_shrink = reduce_rows(shrink_grad)
    total_expand = reduce_columns(expand_grad, 1)
    total_output = reduce_rows(output_grad)
    total_input = reduce_columns(input_grad, 3)

    half_width = width // 2
    table_vector = gather_table(table_grad, GRID)
    split_vector = jnp.concatenate(
        [
            table_vector.reshape(-1),
            projected_bias_grad[0, :half_width],
            projected_bias_grad[0, 2 * half_width :],
            expand_bias_grad[0],
        ]
    )
    both_vector = jnp.concatenate([sums_two[3], shrink_bias_grad[0]])
    split_rows = -(-split_vector.shape[0] // LANES)
    split_vector_padded = jnp.pad(split_vector, (0, split_rows * LANES - split_vector.shape[0]))
    small = jnp.concatenate([split_vector_padded, both_vector]).reshape(-1, LANES)
    small = small + swap_core(small)
    for bit in group_bits():
        small = small + swap_group(small, bit)
    small_own = small[:split_rows]
    small_two = ordered(small_own[None], swap_chip(small_own)[None], chip).reshape(2, -1)
    table_size = table_vector.size
    table_total = small_two[:, :table_size].reshape(heads_all, -1).T
    at = table_size
    bias_query = small_two[:, at : at + half_width]
    bias_value = small_two[:, at + half_width : at + 2 * half_width]
    at = at + 2 * half_width
    bias_expand = small_two[:, at : at + feed_width // 2].reshape(-1)
    bias_input = jnp.stack([bias_query, bias_value]).reshape(-1)
    both = small[split_rows:].reshape(2, width)

    def own_part(vector):
        size = vector.shape[0] // 4
        return lax.dynamic_slice_in_dim(vector, block * size, size, 0)

    split_sums = jnp.stack([sums_one[0], sums_one[1], grad_gate_two]).reshape(-1, LANES)
    split_sums = (split_sums + swap_chip(split_sums)).reshape(3, width)
    image_row = jnp.concatenate(
        [
            split_sums[0],
            split_sums[1],
            sums_two[2],
            sums_two[0],
            sums_two[1],
            split_sums[2],
            pick(condition, core).astype(F32),
        ]
    ).astype(LOW)
    rows = image_row.reshape(1, -1, LANES)
    rows = ordered(rows, swap_core(rows), core)
    for bit in group_bits():
        rows = ordered(rows, swap_group(rows, bit), bit_of(bit))
    rows = rows.reshape(rows.shape[0], -1)
    grads_all, conditions = rows[:, : 6 * width], rows[:, 6 * width :]
    conditions_own = lax.dynamic_slice_in_dim(conditions, block * own_rows, own_rows, 1)
    modulate_grad = dot(conditions_own, grads_all, 0, 0)
    modulate_bias_grad = own_part(jnp.sum(grads_all.astype(F32), axis=0))

    return (
        result,
        grad_images,
        total_input,
        own_part(bias_input),
        total_output,
        own_part(both[0]),
        total_expand,
        own_part(bias_expand),
        total_shrink,
        own_part(both[1]),
        modulate_grad,
        modulate_bias_grad,
        table_total,
    )


def solution(mesh):
    return jax.shard_map(
        shards,
        mesh=mesh,
        in_specs=(
            P("grp", "blk", None),
            P("grp", "blk", None),
            P("grp"),
            P("blk", None),
            P(),
            P("blk", None),
            P(),
            P("blk", None),
            P(),
            P("blk", None),
            P(),
            P("blk", None),
            P(),
            P(),
        ),
        out_specs=(
            P("grp", "blk", None),
            P("grp", "blk", None),
            P("blk", None),
            P("blk"),
            P("blk", None),
            P("blk"),
            P("blk", None),
            P("blk"),
            P("blk", None),
            P("blk"),
            P("blk", None),
            P("blk"),
            P(),
        ),
        check_vma=False,
    )
```

```python
import functools
import math

import jax
import jax.numpy as jnp
from jax import lax
from jax.experimental import pallas as pl
from jax.experimental.pallas import tpu as pltpu
from jax.sharding import PartitionSpec as P

GRID = 32
F32 = jnp.float32
LOW = jnp.bfloat16
TILE = 256
LANES = 128
MIB = 2**20
FEED_CHUNK = 1152
SHARES = 1
COST = 5e9


def dot(left, right, left_dim, right_dim):
    return lax.dot_general(
        left, right, (((left_dim,), (right_dim,)), ((), ())), preferred_element_type=F32
    )


def call(kernel, grid, in_specs, out_specs, out_shape, scratch=(), mib=56, us=5.0):
    return pl.pallas_call(
        kernel,
        grid_spec=pltpu.PrefetchScalarGridSpec(
            num_scalar_prefetch=1,
            grid=grid,
            in_specs=in_specs,
            out_specs=out_specs,
            scratch_shapes=list(scratch),
        ),
        out_shape=out_shape,
        cost_estimate=pl.CostEstimate(
            flops=int(us * COST), bytes_accessed=1024, transcendentals=0
        ),
        compiler_params=pltpu.CompilerParams(vmem_limit_bytes=mib * MIB),
    )


def shape(dims, kind=F32):
    return jax.ShapeDtypeStruct(dims, kind)


def whole(dims):
    return pl.BlockSpec(dims, lambda *_: (0,) * len(dims))


def tiles(width, index=lambda i, place: i):
    return pl.BlockSpec((TILE, width), lambda i, place: (index(i, place), 0))


BLOCK, CHIP, CORE = 0, 1, 2


def norm_rows(values):
    centered = values - jnp.mean(values, axis=-1, keepdims=True)
    variance = jnp.mean(centered * centered, axis=-1, keepdims=True)
    inverse = lax.rsqrt(variance + 1e-06)
    return centered * inverse, inverse


def norm_back(grad_normed, normed, inverse):
    first = jnp.mean(grad_normed, axis=-1, keepdims=True)
    second = jnp.mean(grad_normed * normed, axis=-1, keepdims=True)
    return inverse * (grad_normed - first - normed * second)


def column_sum(values):
    return jnp.sum(values.astype(F32), axis=0, keepdims=True)


def gather_rows(block, pieces, out_ref):
    rows = pieces[0].shape[0]
    for r, piece in enumerate(pieces):
        start = pl.multiple_of((block ^ r) * rows, 32)
        out_ref[pl.ds(start, rows), :] = piece[...]


def pack_kernel(parts, place_ref, w_ref, mine_ref, other_ref):
    half = w_ref.shape[1] // (2 * parts)
    for chip in range(2):

        @pl.when(place_ref[CHIP] == chip)
        def _(chip=chip):
            for part in range(parts):
                for out_ref, side in ((mine_ref, chip), (other_ref, 1 - chip)):
                    start = (2 * part + side) * half
                    out_ref[:, part * half : (part + 1) * half] = w_ref[:, start : start + half]


def pack_input(place, weight):
    rows, columns = weight.shape
    out = (rows, columns // 2)
    return call(
        functools.partial(pack_kernel, 3),
        (1,),
        [whole(weight.shape)],
        [whole(out)] * 2,
        [shape(out, LOW)] * 2,
        us=3.0,
    )(place, weight)


def pack_feed_kernel(place_ref, out_ref, own_ref, mine_ref):
    mine_ref[...] = jnp.where(pl.program_id(0) == 0, out_ref[...], own_ref[...])


def pack_feed(place, out_weight, expand_weight):
    rows, width = out_weight.shape
    return call(
        pack_feed_kernel,
        (3,),
        [
            whole(out_weight.shape),
            pl.BlockSpec(
                (rows, width), lambda i, place: (0, jnp.maximum(i - 1, 0) ^ place[BLOCK])
            ),
        ],
        pl.BlockSpec((rows, width), lambda i, place: (0, i)),
        shape((rows, 3 * width), LOW),
        us=3.0,
    )(place, out_weight, expand_weight)


def spread_kernel(side, place_ref, upper_ref, lower_ref, o_ref):
    row = lax.broadcasted_iota(jnp.int32, (side, LANES), 0)
    lane = lax.broadcasted_iota(jnp.int32, (side, LANES), 1) % side
    for line in range(upper_ref.shape[1]):
        upper = jnp.broadcast_to(upper_ref[0, line : line + 1], (side, LANES))
        lower = jnp.broadcast_to(lower_ref[0, line : line + 1], (side, LANES))
        upper = pltpu.roll(upper, 0, 1, stride=1, stride_axis=0)
        lower = pltpu.roll(lower, LANES - side, 1, stride=1, stride_axis=0)
        o_ref[0, line * side : (line + 1) * side] = jnp.where(lane >= row, upper, lower)


def spread_table(place, upper, lower, side):
    heads, count, _ = upper.shape
    block = pl.BlockSpec((1, count, LANES), lambda i, place: (i, 0, 0))
    return call(
        functools.partial(spread_kernel, side),
        (heads,),
        [block, block],
        pl.BlockSpec((1, count * side, LANES), lambda i, place: (i, 0, 0)),
        shape((heads, count * side, LANES)),
        us=6.0,
    )(place, upper, lower)


def fold_kernel(side, place_ref, g_ref, upper_ref, lower_ref):
    count = upper_ref.shape[1]
    lane = lax.broadcasted_iota(jnp.int32, (count, LANES), 1) % side
    for head in range(g_ref.shape[0]):
        upper = jnp.zeros((count, LANES), F32)
        every = jnp.zeros((count, LANES), F32)
        for row in range(side):
            line = g_ref[head, pl.ds(row, count, stride=side), :]
            if row:
                line = pltpu.roll(line, LANES - row, 1)
            every = every + line
            upper = upper + jnp.where(lane + row < side, line, 0.0)
        upper_ref[head] = upper
        lower_ref[head] = pltpu.roll(every - upper, side, 1)


def fold_table(place, grads, side):
    heads, rows, _ = grads.shape
    out = (heads, rows // side, LANES)
    return call(
        functools.partial(fold_kernel, side),
        (1,),
        [whole(grads.shape)],
        [whole(out)] * 2,
        [shape(out)] * 2,
        us=3.0,
    )(place, grads)


def project_kernel(
    parts,
    head_dim,
    place_ref,
    x0_ref,
    x1_ref,
    x2_ref,
    x3_ref,
    mod_ref,
    w0_ref,
    w1_ref,
    w2_ref,
    w3_ref,
    b_ref,
    x_ref,
    h_ref,
    o_ref,
    w_ref,
):
    step = pl.program_id(0)

    @pl.when(step == 0)
    def _():
        gather_rows(place_ref[BLOCK], (w0_ref, w1_ref, w2_ref, w3_ref), w_ref)

    piece = step ^ (2 * place_ref[CHIP])
    for r, ref in enumerate((x0_ref, x1_ref, x2_ref, x3_ref)):

        @pl.when(piece == r)
        def _(ref=ref):
            x_ref[...] = ref[...]

    normed, _ = norm_rows(x_ref[...].astype(F32))
    hidden = (normed * (1.0 + mod_ref[1:2]) + mod_ref[0:1]).astype(LOW)
    h_ref[...] = hidden
    low = (dot(hidden, w_ref[...], 1, 0) + b_ref[...]).astype(LOW)
    for part in range(parts):
        o_ref[part] = low[:, part * head_dim : (part + 1) * head_dim]


def project(place, pieces, mod, weights, bias, head_dim):
    width = pieces[0].shape[1]
    count = 4 * TILE
    columns = weights[0].shape[1]
    parts = columns // head_dim
    return call(
        functools.partial(project_kernel, parts, head_dim),
        (4,),
        [whole((TILE, width))] * 4
        + [whole(mod.shape)]
        + [whole(weights[0].shape)] * 4
        + [whole((1, columns))],
        [
            tiles(width),
            tiles(width),
            pl.BlockSpec((parts, TILE, head_dim), lambda i, place: (0, i, 0)),
        ],
        [
            shape((count, width), LOW),
            shape((count, width), LOW),
            shape((parts, count, head_dim), LOW),
        ],
        [pltpu.VMEM((width, columns), LOW)],
        us=12.0,
    )(place, *pieces, mod, *weights, bias)


def table_starts(core, tile, keys):
    last = keys // LANES - 1
    per = TILE // LANES
    starts = []
    for piece in range(per):
        row = []
        for key_tile in range(keys // TILE):
            apart = (key_tile ^ core) - (tile ^ core)
            row.append((last - piece + apart * per) * LANES)
        starts.append(row)
    return starts


def bias_tile(table_ref, head, starts):
    return jnp.concatenate(
        [
            jnp.concatenate([table_ref[head, start : start + TILE, :] for start in row], axis=0)
            for row in starts
        ],
        axis=1,
    )


def on_core(place_ref, body):
    for core in range(2):
        pl.when(place_ref[CORE] == core)(functools.partial(body, core))


def attend_kernel(first_tile, place_ref, *refs):
    on_core(place_ref, lambda core: attend_body(first_tile, core, *refs))


def attend_body(first_tile, core, q_ref, k_ref, v_ref, table_ref, o_ref, lse_ref):
    heads, count, head_dim = q_ref.shape
    scale = head_dim ** (-0.5)
    for tile in range(count // TILE):
        outs, logs = [], []
        starts = table_starts(core, first_tile + tile, k_ref.shape[1])
        span = slice(tile * TILE, (tile + 1) * TILE)
        for head in range(heads):
            scores = dot(k_ref[head], q_ref[head, span, :], 1, 1) * scale
            scores = scores + bias_tile(table_ref, head, starts)
            largest = jnp.max(scores, axis=0, keepdims=True)
            exponent = jnp.exp(scores - largest)
            total = jnp.sum(exponent, axis=0, keepdims=True)
            out = dot(v_ref[head], exponent.astype(LOW), 0, 0)
            outs.append(out / total)
            logs.append(largest + jnp.log(total))
        o_ref[:, span] = jnp.concatenate(outs, axis=0).astype(LOW)
        lse_ref[0, :, span] = jnp.concatenate(logs, axis=0)


def attend(place, parts, table, heads, pair, half):
    _, count, head_dim = parts.shape
    groups = heads // pair
    part_count = count // 2

    def head_block(first):
        return pl.BlockSpec(
            (pair, count, head_dim), lambda i, place, first=first: (first * groups + i, 0, 0)
        )

    return call(
        functools.partial(attend_kernel, half * (part_count // TILE)),
        (groups,),
        [
            pl.BlockSpec((pair, part_count, head_dim), lambda i, place: (i, half, 0)),
            head_block(1),
            head_block(2),
            pl.BlockSpec((pair,) + table.shape[1:], lambda i, place: (i, 0, 0)),
        ],
        [
            pl.BlockSpec((pair * head_dim, part_count), lambda i, place: (i, 0)),
            pl.BlockSpec((1, pair, part_count), lambda i, place: (i, 0, 0)),
        ],
        [shape((heads * head_dim, part_count), LOW), shape((groups, pair, part_count))],
        us=14.0,
    )(place, parts, parts, parts, table)


def attend_back_kernel(place_ref, *refs):
    on_core(place_ref, lambda core: attend_back_body(core, *refs))


def attend_back_body(
    core,
    q_ref,
    k_ref,
    v_ref,
    go0_ref,
    go1_ref,
    o0_ref,
    o1_ref,
    lse0_ref,
    lse1_ref,
    table_ref,
    gq_ref,
    gk_ref,
    gv_ref,
    gt_ref,
):
    heads, count, head_dim = q_ref.shape
    keys = k_ref.shape[1]
    scale = head_dim ** (-0.5)
    half_tiles = count // TILE // 2
    gt_ref[...] = jnp.zeros_like(gt_ref)
    for head in range(heads):
        key = k_ref[head]
        value = v_ref[head]
        grad_key = jnp.zeros((keys, head_dim), F32)
        grad_value = jnp.zeros((keys, head_dim), F32)
        for tile in range(count // TILE):
            go_ref, o_ref, lse_ref = (
                (go0_ref, o0_ref, lse0_ref) if tile < half_tiles else (go1_ref, o1_ref, lse1_ref)
            )
            inner = slice((tile % half_tiles) * TILE, (tile % half_tiles + 1) * TILE)
            span = slice(tile * TILE, (tile + 1) * TILE)
            starts = table_starts(core, tile, keys)
            query = q_ref[head, span, :]
            grad_out = go_ref[head, inner, :]
            scores = dot(key, query, 1, 1) * scale + bias_tile(table_ref, head, starts)
            probs = jnp.exp(scores - lse_ref[0, head : head + 1, inner])
            grad_probs = dot(value, grad_out, 1, 1)
            out = o_ref[head * head_dim : (head + 1) * head_dim, inner].astype(F32)
            row_dot = jnp.sum(out * grad_out.astype(F32).T, axis=0, keepdims=True)
            grad_scores = probs * (grad_probs - row_dot)
            for piece, row in enumerate(starts):
                for key_tile, start in enumerate(row):
                    gt_ref[head, start : start + TILE, :] += grad_scores[
                        key_tile * TILE : (key_tile + 1) * TILE,
                        piece * LANES : (piece + 1) * LANES,
                    ]
            low = grad_scores.astype(LOW)
            grad_value = grad_value + dot(probs.astype(LOW), grad_out, 1, 0)
            grad_key = grad_key + dot(low, query, 1, 0)
            gq_ref[head, span, :] = (dot(key, low, 0, 0) * scale).T.astype(LOW)
        gk_ref[head] = (grad_key * scale).astype(LOW)
        gv_ref[head] = grad_value.astype(LOW)


def attend_back(place, parts, grad_outs, attended, logs, table, heads, pair, share, at):
    _, count, head_dim = parts.shape
    groups = heads // pair
    steps = share // pair
    half = count // 2

    def head_block(first, rows=count):
        return pl.BlockSpec(
            (pair, rows, head_dim),
            lambda i, place: (first * groups + at * steps + i, 0, 0),
        )

    out_block = pl.BlockSpec((pair, count, head_dim), lambda i, place: (i, 0, 0))
    attended_block = pl.BlockSpec(
        (pair * head_dim, half), lambda i, place: (at * steps + i, 0)
    )
    log_block = pl.BlockSpec((1, pair, half), lambda i, place: (at * steps + i, 0, 0))
    table_dims = (pair,) + table.shape[1:]
    return call(
        attend_back_kernel,
        (steps,),
        [head_block(0), head_block(1), head_block(2)]
        + [head_block(0, half)] * 2
        + [attended_block] * 2
        + [log_block] * 2
        + [pl.BlockSpec(table_dims, lambda i, place: (at * steps + i, 0, 0))],
        [out_block] * 3 + [pl.BlockSpec(table_dims, lambda i, place: (i, 0, 0))],
        [shape((share, count, head_dim), LOW)] * 3 + [shape((share,) + table.shape[1:])],
        us=14.0,
    )(place, parts, parts, parts, *grad_outs, *attended, *logs, table)


def middle_kernel(
    first_tile,
    place_ref,
    own_ref,
    got_ref,
    w0_ref,
    w1_ref,
    w2_ref,
    w3_ref,
    ob_ref,
    x_ref,
    c0_ref,
    c1_ref,
    c2_ref,
    c3_ref,
    mod_ref,
    br_ref,
    mid_ref,
    h_ref,
    gb_ref,
    cot_ref,
    sum_ref,
    w_ref,
):
    step = pl.program_id(0)

    @pl.when(step == 0)
    def _():
        rows = w0_ref.shape[0]
        core = place_ref[CORE]
        for r, piece in enumerate((w0_ref, w1_ref, w2_ref, w3_ref)):
            start = pl.multiple_of(((core ^ (r % 2)) + 2 * (r // 2)) * rows, 32)
            w_ref[pl.ds(start, rows), :] = piece[...]
        sum_ref[...] = jnp.zeros_like(sum_ref)

    piece = (step + first_tile) ^ (2 * place_ref[CHIP])
    for r, ref in enumerate((c0_ref, c1_ref, c2_ref, c3_ref)):

        @pl.when(piece == r)
        def _(ref=ref):
            cot_ref[...] = ref[...]

    joined = jnp.concatenate([own_ref[...], got_ref[...]], axis=0)
    branch = dot(joined, w_ref[...], 0, 0) + ob_ref[...]
    middle = x_ref[...].astype(F32) + mod_ref[2:3] * branch
    normed, _ = norm_rows(middle)
    br_ref[...] = branch.astype(LOW)
    mid_ref[...] = middle
    h_ref[...] = (normed * (1.0 + mod_ref[4:5]) + mod_ref[3:4]).astype(LOW)
    grad = (mod_ref[5:6] * cot_ref[...].astype(F32)).astype(LOW)
    gb_ref[...] = grad
    sum_ref[...] += column_sum(grad)


def middle_part(place, own, got, weights, bias, tokens, cotangents, mod, half):
    width = tokens.shape[1]
    rows, count = own.shape
    first = half * (count // TILE)
    low, full = shape((count, width), LOW), shape((count, width))
    side = pl.BlockSpec((rows, TILE), lambda i, place: (0, i))
    return call(
        functools.partial(middle_kernel, first),
        (count // TILE,),
        [side, side]
        + [whole((width // 4, width))] * 4
        + [whole((1, width)), tiles(width, lambda i, place: i + first)]
        + [whole((TILE, width))] * 4
        + [whole(mod.shape)],
        [tiles(width)] * 5 + [whole((1, width))],
        [low, full, low, low, low, shape((1, width))],
        [pltpu.VMEM((width, width), LOW)],
        us=7.0,
    )(place, own, got, *weights, bias, tokens, *cotangents, mod)


def feed_kernel(
    place_ref,
    h_ref,
    g_ref,
    e0_ref,
    e1_ref,
    e2_ref,
    e3_ref,
    s0_ref,
    s1_ref,
    be_ref,
    act_ref,
    ge_ref,
    sum_ref,
    b2_ref,
    gh_ref,
    we_ref,
    b2_acc,
    gh_acc,
):
    step = pl.program_id(0)
    steps = pl.num_programs(0)
    gather_rows(place_ref[BLOCK], (e0_ref, e1_ref, e2_ref, e3_ref), we_ref)
    expand = we_ref[...]
    hidden, grad = h_ref[...], g_ref[...]
    shrink = jnp.where(step < steps // 2, s0_ref[...], s1_ref[...])
    inner = dot(hidden, expand, 1, 0) + be_ref[...]
    slope = math.sqrt(2.0 / math.pi)
    square = inner * inner
    bent = jnp.tanh(slope * (inner + 0.044715 * inner * square))
    act = (0.5 * inner * (1.0 + bent)).astype(LOW)
    act_ref[...] = act
    back = 0.5 * (1.0 + bent) + 0.5 * inner * (1.0 - bent * bent) * (
        slope * (1.0 + 3 * 0.044715 * square)
    )
    grad_inner = (dot(grad, shrink, 1, 1) * back).astype(LOW)
    ge_ref[...] = grad_inner
    sum_ref[...] = column_sum(grad_inner)

    @pl.when(step == 0)
    def _():
        b2_acc[...] = dot(act, shrink, 1, 0)
        gh_acc[...] = dot(grad_inner, expand, 1, 1)

    @pl.when(step > 0)
    def _():
        b2_acc[...] += dot(act, shrink, 1, 0)
        gh_acc[...] += dot(grad_inner, expand, 1, 1)

    @pl.when(step == steps - 1)
    def _():
        b2_ref[...] = b2_acc[...].astype(LOW)
        gh_ref[...] = gh_acc[...].astype(LOW)


def feed(place, hidden, grad, expands, shrinks, bias, chunk):
    count, width = hidden.shape
    rows = expands[0].shape[0]
    inner = 2 * shrinks[0].shape[0]
    steps = inner // chunk
    half = steps // 2
    skip = width // chunk
    straight = pl.BlockSpec((rows, chunk), lambda i, place: (0, i + skip))
    swapped = pl.BlockSpec((rows, chunk), lambda i, place: (0, (i + half) % steps + skip))
    columns = pl.BlockSpec((count, chunk), lambda i, place: (0, i))
    return call(
        feed_kernel,
        (steps,),
        [
            whole(hidden.shape),
            whole(grad.shape),
            straight,
            swapped,
            straight,
            swapped,
            pl.BlockSpec((chunk, width), lambda i, place: (jnp.minimum(i, half - 1), 0)),
            pl.BlockSpec((chunk, width), lambda i, place: (jnp.maximum(i - half, 0), 0)),
            pl.BlockSpec((1, chunk), lambda i, place: (0, i)),
        ],
        [
            columns,
            columns,
            pl.BlockSpec((1, chunk), lambda i, place: (0, i)),
            whole((count, width)),
            whole((count, width)),
        ],
        [
            shape((count, inner), LOW),
            shape((count, inner), LOW),
            shape((1, inner)),
            shape((count, width), LOW),
            shape((count, width), LOW),
        ],
        [pltpu.VMEM((width, chunk), LOW)] + [pltpu.VMEM((count, width), F32)] * 2,
        us=22.0,
    )(place, hidden, grad, *expands, *shrinks, bias)


def shrink_grad_kernel(place_ref, a0_ref, a1_ref, g0_ref, g1_ref, o_ref):
    total = dot(a0_ref[...], g0_ref[...], 0, 0) + dot(a1_ref[...], g1_ref[...], 0, 0)
    o_ref[...] = total.astype(LOW)


def shrink_grad(place, acts, grads, half, chunk=384):
    count, inner = acts[0].shape
    width = grads[0].shape[1]
    steps = inner // 2 // chunk
    columns = pl.BlockSpec((count, chunk), lambda i, place: (0, i + half * steps))
    return call(
        shrink_grad_kernel,
        (steps,),
        [columns] * 2 + [whole((count, width))] * 2,
        pl.BlockSpec((chunk, width), lambda i, place: (i, 0)),
        shape((inner // 2, width), LOW),
        us=5.0,
    )(place, *acts, *grads)


def expand_grad_kernel(place_ref, h0_ref, h1_ref, g0_ref, g1_ref, *refs):
    keeps, sends, acc_ref = refs[:2], refs[2:4], refs[4]
    acc_ref[...] = dot(h0_ref[...], g0_ref[...], 0, 0) + dot(h1_ref[...], g1_ref[...], 0, 0)
    rows = keeps[0].shape[0]
    for r in range(4):
        start = pl.multiple_of((place_ref[BLOCK] ^ r) * rows, 32)
        out_ref = (sends if r % 2 else keeps)[r // 2]
        out_ref[...] = acc_ref[pl.ds(start, rows), :].astype(LOW)


def expand_grad(place, hiddens, grads, chunk=384):
    count, width = hiddens[0].shape
    inner = grads[0].shape[1]
    steps = inner // chunk
    half = steps // 2
    rows = width // 4
    straight = pl.BlockSpec((rows, chunk), lambda i, place: (0, i))
    swapped = pl.BlockSpec((rows, chunk), lambda i, place: (0, (i + half) % steps))
    return call(
        expand_grad_kernel,
        (steps,),
        [whole((count, width))] * 2 + [pl.BlockSpec((count, chunk), lambda i, place: (0, i))] * 2,
        [straight] * 2 + [swapped] * 2,
        [shape((rows, inner), LOW)] * 4,
        [pltpu.VMEM((width, chunk), F32)],
        us=10.0,
    )(place, *hiddens, *grads)


def input_grad_kernel(place_ref, h_ref, gq_ref, gk_ref, gv_ref, *refs):
    step = pl.program_id(0)
    chunk = h_ref.shape[1]
    heads, _, head_dim = gq_ref.shape
    columns = 3 * heads * head_dim
    keep_ref, send_ref, joined_ref, acc_ref = refs[-4:]

    @pl.when(step == 0)
    def _():
        for side, ref in enumerate((gq_ref, gk_ref, gv_ref)):
            for head in range(heads):
                start = (side * heads + head) * head_dim
                joined_ref[:, start : start + head_dim] = ref[head]

    total = dot(h_ref[...], joined_ref[...], 0, 0)
    acc_ref[pl.ds(pl.multiple_of(step * chunk, chunk), chunk), :] = total

    @pl.when(step == pl.num_programs(0) - 1)
    def _():
        rows = keep_ref.shape[0]
        block = place_ref[BLOCK]
        for r in range(4):
            start = pl.multiple_of((block ^ r) * rows, 32)
            out_ref = send_ref if r % 2 else keep_ref
            at = (r // 2) * columns
            out_ref[:, at : at + columns] = acc_ref[pl.ds(start, rows), :].astype(LOW)

    if len(refs) > 4:
        a0_ref, a1_ref, g0_ref, g1_ref = refs[:4]

        @pl.when(step == 0)
        def _():
            out = dot(a0_ref[...], g0_ref[...], 1, 0) + dot(a1_ref[...], g1_ref[...], 1, 0)
            rows = keep_ref.shape[0]
            first, second = out[:rows].astype(LOW), out[rows:].astype(LOW)
            own = place_ref[CORE] == 0
            keep_ref[:, 2 * columns :] = jnp.where(own, first, second)
            send_ref[:, 2 * columns :] = jnp.where(own, second, first)


def input_grad(place, hidden, grads, extra=(), chunk=384):
    heads, count, head_dim = grads[0].shape
    width = hidden.shape[1]
    columns = 3 * heads * head_dim
    more = [*extra[0], *extra[1]] if extra else []
    out = (width // 4, 2 * columns + (width if extra else 0))
    return call(
        input_grad_kernel,
        (width // chunk,),
        [pl.BlockSpec((count, chunk), lambda i, place: (0, i))]
        + [whole((heads, count, head_dim))] * 3
        + [whole(one.shape) for one in more],
        [whole(out)] * 2,
        [shape(out, LOW)] * 2,
        [pltpu.VMEM((count, columns), LOW), pltpu.VMEM((width, columns), F32)],
        us=9.0 if extra else 6.0,
    )(place, hidden, *grads, *more)


def branch_back_kernel(
    head_dim,
    place_ref,
    own_ref,
    got_ref,
    mid_ref,
    cot_ref,
    br_ref,
    w0_ref,
    w1_ref,
    mod_ref,
    gm_ref,
    gb_ref,
    ga_ref,
    sum_ref,
    w_ref,
):
    @pl.when(pl.program_id(0) == 0)
    def _():
        rows = w0_ref.shape[0]
        core = place_ref[CORE]
        w_ref[pl.ds(pl.multiple_of(core * rows, 32), rows), :] = w0_ref[...]
        w_ref[pl.ds(pl.multiple_of((1 - core) * rows, 32), rows), :] = w1_ref[...]
        sum_ref[...] = jnp.zeros_like(sum_ref)

    grad_hidden = own_ref[...].astype(F32) + got_ref[...].astype(F32)
    normed, inverse = norm_rows(mid_ref[...])
    grad_middle = cot_ref[...].astype(F32) + norm_back(
        grad_hidden * (1.0 + mod_ref[4:5]), normed, inverse
    )
    gm_ref[...] = grad_middle
    grad_branch = (mod_ref[2:3] * grad_middle).astype(LOW)
    gb_ref[...] = grad_branch
    grad_att = dot(grad_branch, w_ref[...], 1, 1).astype(LOW)
    for part in range(ga_ref.shape[0]):
        ga_ref[part] = grad_att[:, part * head_dim : (part + 1) * head_dim]
    sum_ref[0:1] += column_sum(grad_hidden)
    sum_ref[1:2] += column_sum(grad_hidden * normed)
    sum_ref[2:3] += column_sum(grad_middle * br_ref[...].astype(F32))
    sum_ref[3:4] += column_sum(grad_branch)


def branch_back(place, own, got, middle, cotangent, branch, weights, mod, head_dim):
    count, width = own.shape
    rows = width // 2
    parts = rows // head_dim
    return call(
        functools.partial(branch_back_kernel, head_dim),
        (count // TILE,),
        [tiles(width)] * 5 + [whole((width // 4, width))] * 2 + [whole(mod.shape)],
        [
            tiles(width),
            tiles(width),
            pl.BlockSpec((parts, TILE, head_dim), lambda i, place: (0, i, 0)),
            whole((8, width)),
        ],
        [
            shape((count, width)),
            shape((count, width), LOW),
            shape((parts, count, head_dim), LOW),
            shape((8, width)),
        ],
        [pltpu.VMEM((rows, width), LOW)],
        us=7.0,
    )(place, own, got, middle, cotangent, branch, *weights, mod)


def project_back_kernel(groups, place_ref, *refs):
    part_refs = refs[: 3 * groups]
    w_refs = refs[3 * groups : 3 * groups + 4]
    x_ref, gh_ref, sum_ref, bias_ref, w_ref = refs[3 * groups + 4 :]

    @pl.when(pl.program_id(0) == 0)
    def _():
        gather_rows(place_ref[BLOCK], w_refs, w_ref)
        sum_ref[...] = jnp.zeros_like(sum_ref)
        bias_ref[...] = jnp.zeros_like(bias_ref)

    pieces = [ref[part] for ref in part_refs for part in range(ref.shape[0])]
    joined = jnp.concatenate(pieces, axis=1)
    grad_hidden = dot(joined, w_ref[...], 1, 1)
    gh_ref[...] = grad_hidden.astype(LOW)
    normed, _ = norm_rows(x_ref[...].astype(F32))
    sum_ref[0:1] += column_sum(grad_hidden)
    sum_ref[1:2] += column_sum(grad_hidden * normed)
    bias_ref[...] += column_sum(joined)


def project_back(place, parts, weights, tokens, far):
    width = tokens.shape[1]
    count = tokens.shape[0] // 2
    columns = weights[0].shape[1]
    pair, _, head_dim = parts[0].shape
    steps = count // TILE

    def index(i, place):
        return (place[CHIP] ^ far) * steps + i

    return call(
        functools.partial(project_back_kernel, len(parts) // 3),
        (steps,),
        [pl.BlockSpec((pair, TILE, head_dim), lambda i, place: (0, index(i, place), 0))]
        * len(parts)
        + [whole(weights[0].shape)] * 4
        + [tiles(width, index)],
        [tiles(width), whole((8, width)), whole((1, columns))],
        [
            shape((count, width), LOW),
            shape((8, width)),
            shape((1, columns)),
        ],
        [pltpu.VMEM((width, columns), LOW)],
        us=7.0,
    )(place, *parts, *weights, tokens)


def input_back_kernel(place_ref, own_ref, got_ref, x_ref, gm0_ref, gm1_ref, mod_ref, o_ref):
    grad_hidden = own_ref[...].astype(F32) + got_ref[...].astype(F32)
    normed, inverse = norm_rows(x_ref[...].astype(F32))
    grad_middle = jnp.where(place_ref[CHIP] == 0, gm0_ref[...], gm1_ref[...])
    grad = grad_middle + norm_back(grad_hidden * (1.0 + mod_ref[1:2]), normed, inverse)
    o_ref[0] = grad.astype(LOW)


def input_back(place, own, got, tokens, grad_middles, mod):
    count, width = own.shape
    steps = count // TILE
    return call(
        input_back_kernel,
        (steps,),
        [tiles(width)] * 2
        + [tiles(width, lambda i, place: place[CHIP] * steps + i)]
        + [tiles(width)] * 2
        + [whole(mod.shape)],
        pl.BlockSpec((1, TILE, width), lambda i, place: (i, 0, 0)),
        shape((steps, TILE, width), LOW),
        us=4.0,
    )(place, own, got, tokens, *grad_middles, mod)


def result_kernel(
    place_ref,
    b0_ref,
    b1_ref,
    got_ref,
    mid0_ref,
    mid1_ref,
    cot0_ref,
    cot1_ref,
    bias_ref,
    mod_ref,
    o_ref,
    sum_ref,
):
    @pl.when(pl.program_id(0) == 0)
    def _():
        sum_ref[...] = jnp.zeros_like(sum_ref)

    def own(one, two):
        return jnp.where(place_ref[CHIP] == 0, one[...].astype(F32), two[...].astype(F32))

    branch = own(b0_ref, b1_ref) + got_ref[...].astype(F32) + bias_ref[...]
    o_ref[0] = (own(mid0_ref, mid1_ref) + mod_ref[5:6] * branch).astype(LOW)
    sum_ref[0:1] += column_sum(own(cot0_ref, cot1_ref) * branch)


def result_part(place, branches, got, middles, cotangents, bias, mod):
    count, width = got.shape
    steps = count // TILE
    return call(
        result_kernel,
        (steps,),
        [tiles(width)] * 7 + [whole((1, width)), whole(mod.shape)],
        [pl.BlockSpec((1, TILE, width), lambda i, place: (i, 0, 0)), whole((8, width))],
        [shape((steps, TILE, width), LOW), shape((8, width))],
        us=4.0,
    )(place, *branches, got, *middles, *cotangents, bias, mod)


def finish_expand_kernel(place_ref, own_ref, far_ref, o_ref):
    near = (pl.program_id(0) ^ place_ref[BLOCK]) < 2
    o_ref[...] = jnp.where(near, own_ref[...].astype(F32), far_ref[...].astype(F32))


def finish_expand(place, own, far):
    rows, columns = own.shape
    width = columns // 2
    block = pl.BlockSpec((rows, width), lambda i, place: (0, (i ^ place[BLOCK]) % 2))
    return call(
        finish_expand_kernel,
        (4,),
        [block, block],
        pl.BlockSpec((rows, width), lambda i, place: (0, i)),
        shape((rows, 2 * columns)),
        us=3.0,
    )(place, own, far)


def finish_input_kernel(place_ref, *refs):
    grads, o_ref = refs[:-1], refs[-1]
    shares = len(grads)
    part_width = o_ref.shape[1] // (6 * shares)
    for chip in range(2):

        @pl.when(place_ref[CHIP] == chip)
        def _(chip=chip):
            for share, g_ref in enumerate(grads):
                for side in range(2):
                    for part in range(3):
                        start = (side * 3 + part) * part_width
                        to = ((part * 2 + (side ^ chip)) * shares + share) * part_width
                        o_ref[:, to : to + part_width] = g_ref[:, start : start + part_width].astype(F32)


def finish_input(place, grads, columns):
    rows = grads[0].shape[0]
    out = (rows, columns)
    return call(
        finish_input_kernel,
        (1,),
        [whole(grad.shape) for grad in grads],
        whole(out),
        shape(out),
        us=3.0,
    )(place, *grads)


def swap_block(value, bits):
    return lax.ppermute(value, "blk", [(i, i ^ bits) for i in range(4)])


def swap_core(value):
    return swap_block(value, 1)


def swap_chip(value):
    return swap_block(value, 2)


def ordered(mine, other, place, axis=0):
    first = jnp.where(place == 0, mine, other)
    second = jnp.where(place == 0, other, mine)
    return jnp.concatenate([first, second], axis=axis)


def add_low(one, two):
    return (one.astype(F32) + two.astype(F32)).astype(LOW)


def stages():
    count = lax.axis_size("grp")
    bits = [1 << i for i in range(count.bit_length() - 1)]
    return [bits[:1]] + [bits[i : i + 2] for i in range(1, len(bits), 2)]


def stage_place(stage):
    at = 0
    for bit in stage:
        own = lax.axis_index("blk") % 2 if bit == 0 else (lax.axis_index("grp") // bit) % 2
        at = 2 * at + own
    return at


def swap_stage(values, stage):
    groups, size = lax.axis_size("grp"), lax.axis_size("blk")
    got = [values[0]]
    for mask in range(1, 1 << len(stage)):
        chosen = [bit for i, bit in enumerate(stage) if mask >> (len(stage) - 1 - i) & 1]
        core_flip = int(0 in chosen)
        group_flip = sum(chosen)
        if group_flip and core_flip:
            pairs = [
                (g * size + i, (g ^ group_flip) * size + (i ^ 1))
                for g in range(groups)
                for i in range(size)
            ]
            got.append(lax.ppermute(values[mask], ("grp", "blk"), pairs))
        elif group_flip:
            pairs = [(g, g ^ group_flip) for g in range(groups)]
            got.append(lax.ppermute(values[mask], "grp", pairs))
        else:
            got.append(swap_core(values[mask]))
    return got


def scatter_stage(value, stage, axis):
    place = stage_place(stage)
    size = value.shape[axis] >> len(stage)
    cut = [
        lax.dynamic_slice_in_dim(value, (place ^ mask) * size, size, axis)
        for mask in range(1 << len(stage))
    ]
    return sum(one.astype(F32) for one in swap_stage(cut, stage)).astype(LOW)


def gather_stage(value, stage, axis=0):
    place = stage_place(stage)
    count = 1 << len(stage)
    got = swap_stage([value] * count, stage)
    parts = []
    for at in range(count):
        part = got[count - 1]
        for mask in range(count - 1):
            part = jnp.where(place == at ^ mask, got[mask], part)
        parts.append(part)
    return jnp.concatenate(parts, axis=axis)


def total_stage(value, stage):
    return sum(swap_stage([value] * (1 << len(stage)), stage))


class Far:
    def __init__(self, share):
        self.value = swap_chip(share)
        self.left = stages()

    @staticmethod
    def share_of(value):
        rows = value.shape[0] // lax.axis_size("grp")
        at = 0
        for stage in stages():
            at = (at << len(stage)) + stage_place(stage)
        return lax.dynamic_slice_in_dim(value, at * rows, rows, 0)

    def gather(self):
        if self.left:
            self.value = gather_stage(self.value, self.left.pop())


def after(value, *others):
    return lax.optimization_barrier((value, *others))[0]


class Sum:
    def __init__(self, keep, send, columns):
        self.value = add_low(keep, swap_core(send))
        self.columns = columns
        self.down = stages()
        self.up = []

    def step(self):
        if self.down:
            stage = self.down.pop(0)
            self.value = scatter_stage(self.value, stage, 0)
            self.up.append(stage)
            if not self.down:
                self.far = swap_chip(self.value[:, self.columns : 2 * self.columns])
        elif self.up:
            if self.far is not None:
                self.value = lax.dynamic_update_slice_in_dim(
                    self.value, self.far, self.columns, 1
                )
                self.far = None
            self.value = gather_stage(self.value, self.up.pop())
        return self.value

    def finish(self):
        while self.down or self.up:
            self.step()
        return self.value


def table_lines(table, side):
    span = 2 * side - 1
    per = LANES // side
    heads = table.shape[1]
    count = 2 * side - per
    flipped = table.T.reshape(heads, span, span)[:, ::-1]
    lines = [flipped[:, per - 1 - k : per - 1 - k + count] for k in range(per)]
    upper = jnp.concatenate([line[:, :, side - 1 :] for line in lines], axis=2)
    lower = jnp.concatenate(
        [jnp.pad(line[:, :, : side - 1], ((0, 0), (0, 0), (1, 0))) for line in lines], axis=2
    )
    return upper, lower


def table_from_lines(upper, lower, side):
    span = 2 * side - 1
    per = LANES // side
    heads, count, _ = upper.shape
    total = 0.0
    for k in range(per):
        line = jnp.concatenate(
            [lower[:, :, k * side + 1 : (k + 1) * side], upper[:, :, k * side : (k + 1) * side]],
            axis=2,
        )
        before = per - 1 - k
        total = total + jnp.pad(line, ((0, 0), (before, span - count - before), (0, 0)))
    return total[:, ::-1].reshape(heads, span * span)


def embedding(step_values, width):
    half_width = width // 2
    frequency = jnp.exp(-math.log(10000.0) * jnp.arange(half_width, dtype=F32) / half_width)
    angles = step_values.astype(F32)[:, None] * frequency[None, :]
    return jnp.concatenate([jnp.cos(angles), jnp.sin(angles)], axis=-1)


def pick(value, place, axis=0):
    return lax.dynamic_index_in_dim(value, place, axis, keepdims=False)


def shards(
    images,
    cotangent,
    timestep,
    input_weight,
    input_bias,
    output_weight,
    output_bias,
    expand_weight,
    expand_bias,
    shrink_weight,
    shrink_bias,
    modulate_weight,
    modulate_bias,
    position_table,
):
    width = images.shape[2]
    heads_all = position_table.shape[1]
    head_dim = width // heads_all
    heads = heads_all // 2
    pair = 2
    own_rows = modulate_weight.shape[0]
    block = lax.axis_index("blk").astype(jnp.int32)
    chip, core = block // 2, block % 2
    place = jnp.stack([block, chip, core])

    condition = jax.nn.silu(embedding(timestep, width)).astype(LOW)
    condition_own = lax.dynamic_slice_in_dim(condition, block * own_rows, own_rows, 1)
    partial = jnp.dot(condition_own, modulate_weight, preferred_element_type=F32)
    partial = partial.reshape(2, -1, LANES)
    partial_mine, partial_other = pick(partial, core), pick(partial, 1 - core)
    summed = (partial_mine + swap_block(partial_other, 1)) + (
        swap_block(partial_mine, 2) + swap_block(partial_other, 3)
    )
    mod = (summed.reshape(-1) + modulate_bias).reshape(6, width)

    out_share, expand_share = Far.share_of(output_weight), Far.share_of(expand_weight)
    far = Far(
        jnp.concatenate(
            [out_share]
            + [
                lax.dynamic_slice_in_dim(expand_share, (block ^ bits) * width, width, 1)
                for bits in (2, 3)
            ],
            axis=1,
        )
    )

    in_mine, in_other = pack_input(place, after(input_weight, partial_mine))
    in_far = swap_chip(in_other)

    def mine_and_other(value):
        return pick(value, core), pick(value, 1 - core)

    token_mine, token_other = mine_and_other(after(images, partial_mine))
    token_pieces = (
        token_mine,
        swap_block(token_other, 1),
        swap_block(token_mine, 2),
        swap_block(token_other, 3),
    )
    in_mine_got = swap_core(after(in_mine, token_pieces[1], summed))
    feed_mine = pack_feed(place, after(output_weight, in_mine), expand_weight)
    feed_mine_got = swap_core(after(feed_mine, in_mine_got))
    far.gather()
    weights_in = (in_mine, in_mine_got, in_far, swap_core(after(in_far, feed_mine_got)))

    def own_half(vector):
        size = vector.shape[0] // 2
        return lax.dynamic_slice_in_dim(vector, chip * size, size, 0)

    bias_in = jnp.concatenate(
        [
            own_half(input_bias[:width]),
            jnp.zeros((width // 2,), F32),
            own_half(input_bias[width:]),
        ]
    )[None]
    expand_bias_blocks = expand_bias.reshape(4, -1)
    bias_expand = jnp.concatenate(
        [pick(expand_bias_blocks, block), pick(expand_bias_blocks, block ^ 1)]
    )[None]
    upper, lower = table_lines(
        lax.dynamic_slice_in_dim(position_table, chip * heads, heads, 1), GRID
    )
    table = spread_table(place, upper, lower, GRID)

    tokens, hidden_one, parts = project(
        place,
        token_pieces,
        after(mod, feed_mine_got, far.value, table),
        weights_in,
        bias_in,
        head_dim,
    )
    far.gather()
    cot_mine, cot_other = mine_and_other(after(cotangent, token_pieces[2], token_pieces[3]))
    cot_pieces = (
        cot_mine,
        swap_block(cot_other, 1),
        swap_block(cot_mine, 2),
        swap_block(cot_other, 3),
    )
    attended, logs = [None, None], [None, None]
    attended[0], logs[0] = attend(
        place, after(parts, cot_pieces[1]), table, heads, pair, 0
    )
    far.gather()
    shrink_got = swap_core(after(shrink_weight, cot_pieces[1]))
    weights_shrink = (shrink_weight, shrink_got)
    attended_got = [swap_chip(attended[0]), None]
    attended[1], logs[1] = attend(
        place, after(parts, shrink_got, far.value, attended[0]), table, heads, pair, 1
    )
    attended_got[1] = swap_chip(attended[1])
    weights_feed = (feed_mine, feed_mine_got, far.value, swap_core(far.value))

    def forward_half(half, attended_half):
        one = middle_part(
            place,
            attended_half,
            attended_got[half],
            weights_feed,
            output_bias[None],
            tokens,
            cot_pieces,
            mod,
            half,
        )
        two = feed(
            place, one[2], one[3], weights_feed, weights_shrink, bias_expand, FEED_CHUNK
        )
        return one + two

    forward = [forward_half(0, attended[0])]
    grad_hidden_two_got = [swap_chip(forward[0][-1])]
    forward.append(forward_half(1, after(attended[1], forward[0][-1])))
    grad_hidden_two_got.append(swap_chip(forward[1][-1]))
    (
        branch_one,
        middle,
        hidden_two,
        grad_branch_two,
        cots,
        shrink_sums,
        activated,
        grad_expanded,
        expand_sums,
        branch_two,
        grad_hidden_two,
    ) = zip(*forward)

    shrink_send = shrink_grad(
        place, (after(activated[0], grad_hidden_two_got[0]), activated[1]), grad_branch_two, 1
    )
    shrink_keep = shrink_grad(place, activated, grad_branch_two, 0)
    shrink_own = add_low(shrink_keep, swap_core(shrink_send))
    expand_keep0, expand_keep1, expand_send0, expand_send1 = expand_grad(
        place, (after(hidden_two[0], shrink_keep), hidden_two[1]), grad_expanded
    )
    expand_own = add_low(expand_keep0, swap_core(expand_send0))
    expand_far = add_low(expand_keep1, swap_core(expand_send1))
    total_shrink, total_own, total_far = lax.psum((shrink_own, expand_own, expand_far), "grp")

    def branch_half(half, *others):
        return branch_back(
            place,
            grad_hidden_two[half],
            grad_hidden_two_got[half],
            after(middle[half], *others),
            cots[half],
            branch_one[half],
            weights_feed[:2],
            mod,
            head_dim,
        )

    grad_middle, grad_branch_one, grad_attended, sums_two = zip(
        branch_half(0, shrink_own), branch_half(1, expand_own, expand_far)
    )
    branch_two_send = jnp.where(chip == 0, branch_two[1], branch_two[0])

    def attend_share(at, *others):
        return attend_back(
            place,
            after(parts, *others),
            grad_attended,
            attended,
            logs,
            table,
            heads,
            pair,
            heads // SHARES,
            at,
        )

    share_columns = width * 3 // (2 * SHARES)
    share = attend_share(0)
    branch_two_got = swap_chip(after(branch_two_send, share[0]))
    keep, send = input_grad(
        place, hidden_one, share[:3], (attended, grad_branch_one), 384
    )
    input_total = Sum(keep, send, share_columns)
    grad_parts, table_grads = share[:3], share[3:]
    grad_hidden_far, sums_far, bias_far = project_back(
        place, grad_parts, weights_in, after(tokens, input_total.value), 1
    )
    input_total.step()
    grad_hidden_got = swap_chip(grad_hidden_far)
    grad_hidden_own, sums_own, bias_own = project_back(
        place, grad_parts, weights_in, after(tokens, grad_hidden_far), 0
    )
    result_half, gate_sums = result_part(
        place,
        branch_two,
        branch_two_got,
        middle,
        cots,
        shrink_bias[None],
        after(mod, grad_hidden_own),
    )
    grad_tokens = input_back(
        place, grad_hidden_own, grad_hidden_got, tokens, grad_middle, mod
    )

    def to_blocks(value):
        return ordered(value[0][None], swap_core(value[1])[None], core)

    result = to_blocks(result_half)
    grad_images = to_blocks(grad_tokens)
    total_shrink = total_shrink.astype(F32)
    total_expand = finish_expand(place, total_own, swap_chip(total_far))
    totals = [input_total.finish()]
    total_input = finish_input(place, totals, 3 * width)
    total_output = totals[0][:, 2 * share_columns :].astype(F32)

    half_width = width // 2
    folded = [fold_table(place, grads, GRID) for grads in table_grads]
    table_vector = table_from_lines(
        jnp.concatenate([one for one, _ in folded]),
        jnp.concatenate([two for _, two in folded]),
        GRID,
    )
    projected_bias = (bias_far + bias_own)[0]
    expand_sum = (expand_sums[0] + expand_sums[1]).reshape(2, -1)
    split_vector = jnp.concatenate(
        [
            table_vector.reshape(-1),
            projected_bias[:half_width],
            projected_bias[2 * half_width :],
            ordered(expand_sum[0], expand_sum[1], core),
        ]
    )
    sums_two = sums_two[0] + sums_two[1]
    both_vector = jnp.concatenate([sums_two[3], (shrink_sums[0] + shrink_sums[1])[0]])
    split_rows = -(-split_vector.shape[0] // LANES)
    split_vector_padded = jnp.pad(split_vector, (0, split_rows * LANES - split_vector.shape[0]))
    small = jnp.concatenate([split_vector_padded, both_vector]).reshape(-1, LANES)
    ends = stages()
    ends[0] = ends[0] + [0]
    for stage in ends:
        small = total_stage(small, stage)
    small_own = small[:split_rows]
    small_two = ordered(small_own[None], swap_chip(small_own)[None], chip).reshape(2, -1)
    table_size = table_vector.size
    table_total = small_two[:, :table_size].reshape(heads_all, -1).T
    at = table_size
    bias_query = small_two[:, at : at + half_width]
    bias_value = small_two[:, at + half_width : at + 2 * half_width]
    at = at + 2 * half_width
    bias_expand_total = small_two[:, at : at + expand_sum.size].reshape(-1)
    bias_input_total = jnp.stack([bias_query, bias_value]).reshape(-1)
    both = small[split_rows:].reshape(2, width)

    def own_part(vector):
        size = vector.shape[0] // 4
        return lax.dynamic_slice_in_dim(vector, block * size, size, 0)

    sums_one = sums_far + sums_own
    split_sums = jnp.stack([sums_one[0], sums_one[1], gate_sums[0]]).reshape(-1, LANES)
    split_sums = (split_sums + swap_chip(split_sums)).reshape(3, width)
    image_row = jnp.concatenate(
        [
            split_sums[0],
            split_sums[1],
            sums_two[2],
            sums_two[0],
            sums_two[1],
            split_sums[2],
            pick(condition, core).astype(F32),
        ]
    ).astype(LOW)
    rows = image_row.reshape(1, -1, LANES)
    for stage in ends:
        rows = gather_stage(rows, stage if 0 in stage else stage[::-1])
    rows = rows.reshape(rows.shape[0], -1)
    grads_all, conditions = rows[:, : 6 * width], rows[:, 6 * width :]
    conditions_own = lax.dynamic_slice_in_dim(conditions, block * own_rows, own_rows, 1)
    modulate_grad = dot(conditions_own, grads_all, 0, 0)
    modulate_bias_grad = own_part(jnp.sum(grads_all.astype(F32), axis=0))

    return (
        result,
        grad_images,
        total_input,
        own_part(bias_input_total),
        total_output,
        own_part(both[0]),
        total_expand,
        own_part(bias_expand_total),
        total_shrink,
        own_part(both[1]),
        modulate_grad,
        modulate_bias_grad,
        table_total,
    )


def solution(mesh):
    return jax.shard_map(
        shards,
        mesh=mesh,
        in_specs=(
            P("grp", "blk", None),
            P("grp", "blk", None),
            P("grp"),
            P("blk", None),
            P(),
            P("blk", None),
            P(),
            P("blk", None),
            P(),
            P("blk", None),
            P(),
            P("blk", None),
            P(),
            P(),
        ),
        out_specs=(
            P("grp", "blk", None),
            P("grp", "blk", None),
            P("blk", None),
            P("blk"),
            P("blk", None),
            P("blk"),
            P("blk", None),
            P("blk"),
            P("blk", None),
            P("blk"),
            P("blk", None),
            P("blk"),
            P(),
        ),
        check_vma=False,
    )
```

```python
import functools
import math

import jax
import jax.numpy as jnp
from jax import lax
from jax.experimental import pallas as pl
from jax.experimental.pallas import tpu as pltpu
from jax.sharding import PartitionSpec as P

GRID = 32
F32 = jnp.float32
LOW = jnp.bfloat16
TILE = 256
LANES = 128
MIB = 2**20
FEED_CHUNK = 1152
SHARES = 1
COST = 5e9


def dot(left, right, left_dim, right_dim):
    return lax.dot_general(
        left, right, (((left_dim,), (right_dim,)), ((), ())), preferred_element_type=F32
    )


def call(kernel, grid, in_specs, out_specs, out_shape, scratch=(), mib=56, us=5.0):
    return pl.pallas_call(
        kernel,
        grid_spec=pltpu.PrefetchScalarGridSpec(
            num_scalar_prefetch=1,
            grid=grid,
            in_specs=in_specs,
            out_specs=out_specs,
            scratch_shapes=list(scratch),
        ),
        out_shape=out_shape,
        cost_estimate=pl.CostEstimate(
            flops=int(us * COST), bytes_accessed=1024, transcendentals=0
        ),
        compiler_params=pltpu.CompilerParams(vmem_limit_bytes=mib * MIB),
    )


def shape(dims, kind=F32):
    return jax.ShapeDtypeStruct(dims, kind)


def whole(dims):
    return pl.BlockSpec(dims, lambda *_: (0,) * len(dims))


def tiles(width, index=lambda i, place: i):
    return pl.BlockSpec((TILE, width), lambda i, place: (index(i, place), 0))


BLOCK, CHIP, CORE = 0, 1, 2


def norm_rows(values):
    centered = values - jnp.mean(values, axis=-1, keepdims=True)
    variance = jnp.mean(centered * centered, axis=-1, keepdims=True)
    inverse = lax.rsqrt(variance + 1e-06)
    return centered * inverse, inverse


def norm_back(grad_normed, normed, inverse):
    first = jnp.mean(grad_normed, axis=-1, keepdims=True)
    second = jnp.mean(grad_normed * normed, axis=-1, keepdims=True)
    return inverse * (grad_normed - first - normed * second)


def column_sum(values):
    return jnp.sum(values.astype(F32), axis=0, keepdims=True)


def gather_rows(block, pieces, out_ref):
    rows = pieces[0].shape[0]
    for r, piece in enumerate(pieces):
        start = pl.multiple_of((block ^ r) * rows, 32)
        out_ref[pl.ds(start, rows), :] = piece[...]


def pack_kernel(parts, place_ref, w_ref, mine_ref, other_ref):
    half = w_ref.shape[1] // (2 * parts)
    for chip in range(2):

        @pl.when(place_ref[CHIP] == chip)
        def _(chip=chip):
            for part in range(parts):
                for out_ref, side in ((mine_ref, chip), (other_ref, 1 - chip)):
                    start = (2 * part + side) * half
                    out_ref[:, part * half : (part + 1) * half] = w_ref[:, start : start + half]


def pack_input(place, weight):
    rows, columns = weight.shape
    out = (rows, columns // 2)
    return call(
        functools.partial(pack_kernel, 3),
        (1,),
        [whole(weight.shape)],
        [whole(out)] * 2,
        [shape(out, LOW)] * 2,
        us=3.0,
    )(place, weight)


def pack_feed_kernel(place_ref, out_ref, own_ref, mine_ref):
    mine_ref[...] = jnp.where(pl.program_id(0) == 0, out_ref[...], own_ref[...])


def pack_feed(place, out_weight, expand_weight):
    rows, width = out_weight.shape
    return call(
        pack_feed_kernel,
        (3,),
        [
            whole(out_weight.shape),
            pl.BlockSpec(
                (rows, width), lambda i, place: (0, jnp.maximum(i - 1, 0) ^ place[BLOCK])
            ),
        ],
        pl.BlockSpec((rows, width), lambda i, place: (0, i)),
        shape((rows, 3 * width), LOW),
        us=3.0,
    )(place, out_weight, expand_weight)


def spread_kernel(side, place_ref, upper_ref, lower_ref, o_ref):
    row = lax.broadcasted_iota(jnp.int32, (side, LANES), 0)
    lane = lax.broadcasted_iota(jnp.int32, (side, LANES), 1) % side
    for line in range(upper_ref.shape[1]):
        upper = jnp.broadcast_to(upper_ref[0, line : line + 1], (side, LANES))
        lower = jnp.broadcast_to(lower_ref[0, line : line + 1], (side, LANES))
        upper = pltpu.roll(upper, 0, 1, stride=1, stride_axis=0)
        lower = pltpu.roll(lower, LANES - side, 1, stride=1, stride_axis=0)
        o_ref[0, line * side : (line + 1) * side] = jnp.where(lane >= row, upper, lower)


def spread_table(place, upper, lower, side):
    heads, count, _ = upper.shape
    block = pl.BlockSpec((1, count, LANES), lambda i, place: (i, 0, 0))
    return call(
        functools.partial(spread_kernel, side),
        (heads,),
        [block, block],
        pl.BlockSpec((1, count * side, LANES), lambda i, place: (i, 0, 0)),
        shape((heads, count * side, LANES)),
        us=6.0,
    )(place, upper, lower)


def fold_kernel(side, place_ref, g_ref, upper_ref, lower_ref):
    count = upper_ref.shape[1]
    lane = lax.broadcasted_iota(jnp.int32, (count, LANES), 1) % side
    for head in range(g_ref.shape[0]):
        upper = jnp.zeros((count, LANES), F32)
        every = jnp.zeros((count, LANES), F32)
        for row in range(side):
            line = g_ref[head, pl.ds(row, count, stride=side), :]
            if row:
                line = pltpu.roll(line, LANES - row, 1)
            every = every + line
            upper = upper + jnp.where(lane + row < side, line, 0.0)
        upper_ref[head] = upper
        lower_ref[head] = pltpu.roll(every - upper, side, 1)


def fold_table(place, grads, side):
    heads, rows, _ = grads.shape
    out = (heads, rows // side, LANES)
    return call(
        functools.partial(fold_kernel, side),
        (1,),
        [whole(grads.shape)],
        [whole(out)] * 2,
        [shape(out)] * 2,
        us=3.0,
    )(place, grads)


def project_kernel(
    parts,
    head_dim,
    place_ref,
    x0_ref,
    x1_ref,
    x2_ref,
    x3_ref,
    mod_ref,
    w0_ref,
    w1_ref,
    w2_ref,
    w3_ref,
    b_ref,
    x_ref,
    h_ref,
    o_ref,
    w_ref,
):
    step = pl.program_id(0)

    @pl.when(step == 0)
    def _():
        gather_rows(place_ref[BLOCK], (w0_ref, w1_ref, w2_ref, w3_ref), w_ref)

    piece = step ^ (2 * place_ref[CHIP])
    for r, ref in enumerate((x0_ref, x1_ref, x2_ref, x3_ref)):

        @pl.when(piece == r)
        def _(ref=ref):
            x_ref[...] = ref[...]

    normed, _ = norm_rows(x_ref[...].astype(F32))
    hidden = (normed * (1.0 + mod_ref[1:2]) + mod_ref[0:1]).astype(LOW)
    h_ref[...] = hidden
    low = (dot(hidden, w_ref[...], 1, 0) + b_ref[...]).astype(LOW)
    for part in range(parts):
        o_ref[part] = low[:, part * head_dim : (part + 1) * head_dim]


def project(place, pieces, mod, weights, bias, head_dim):
    width = pieces[0].shape[1]
    count = 4 * TILE
    columns = weights[0].shape[1]
    parts = columns // head_dim
    return call(
        functools.partial(project_kernel, parts, head_dim),
        (4,),
        [whole((TILE, width))] * 4
        + [whole(mod.shape)]
        + [whole(weights[0].shape)] * 4
        + [whole((1, columns))],
        [
            tiles(width),
            tiles(width),
            pl.BlockSpec((parts, TILE, head_dim), lambda i, place: (0, i, 0)),
        ],
        [
            shape((count, width), LOW),
            shape((count, width), LOW),
            shape((parts, count, head_dim), LOW),
        ],
        [pltpu.VMEM((width, columns), LOW)],
        us=12.0,
    )(place, *pieces, mod, *weights, bias)


def table_starts(core, tile, keys):
    last = keys // LANES - 1
    per = TILE // LANES
    starts = []
    for piece in range(per):
        row = []
        for key_tile in range(keys // TILE):
            apart = (key_tile ^ core) - (tile ^ core)
            row.append((last - piece + apart * per) * LANES)
        starts.append(row)
    return starts


def bias_tile(table_ref, head, starts):
    return jnp.concatenate(
        [
            jnp.concatenate([table_ref[head, start : start + TILE, :] for start in row], axis=0)
            for row in starts
        ],
        axis=1,
    )


def on_core(place_ref, body):
    for core in range(2):
        pl.when(place_ref[CORE] == core)(functools.partial(body, core))


def attend_kernel(first_tile, place_ref, *refs):
    on_core(place_ref, lambda core: attend_body(first_tile, core, *refs))


def attend_body(first_tile, core, q_ref, k_ref, v_ref, table_ref, o_ref, lse_ref):
    heads, count, head_dim = q_ref.shape
    scale = head_dim ** (-0.5)
    for tile in range(count // TILE):
        outs, logs = [], []
        starts = table_starts(core, first_tile + tile, k_ref.shape[1])
        span = slice(tile * TILE, (tile + 1) * TILE)
        for head in range(heads):
            scores = dot(k_ref[head], q_ref[head, span, :], 1, 1) * scale
            scores = scores + bias_tile(table_ref, head, starts)
            largest = jnp.max(scores, axis=0, keepdims=True)
            exponent = jnp.exp(scores - largest)
            total = jnp.sum(exponent, axis=0, keepdims=True)
            out = dot(v_ref[head], exponent.astype(LOW), 0, 0)
            outs.append(out / total)
            logs.append(largest + jnp.log(total))
        o_ref[:, span] = jnp.concatenate(outs, axis=0).astype(LOW)
        lse_ref[0, :, span] = jnp.concatenate(logs, axis=0)


def attend(place, parts, table, heads, pair, half):
    _, count, head_dim = parts.shape
    groups = heads // pair
    part_count = count // 2

    def head_block(first):
        return pl.BlockSpec(
            (pair, count, head_dim), lambda i, place, first=first: (first * groups + i, 0, 0)
        )

    return call(
        functools.partial(attend_kernel, half * (part_count // TILE)),
        (groups,),
        [
            pl.BlockSpec((pair, part_count, head_dim), lambda i, place: (i, half, 0)),
            head_block(1),
            head_block(2),
            pl.BlockSpec((pair,) + table.shape[1:], lambda i, place: (i, 0, 0)),
        ],
        [
            pl.BlockSpec((pair * head_dim, part_count), lambda i, place: (i, 0)),
            pl.BlockSpec((1, pair, part_count), lambda i, place: (i, 0, 0)),
        ],
        [shape((heads * head_dim, part_count), LOW), shape((groups, pair, part_count))],
        us=14.0,
    )(place, parts, parts, parts, table)


def attend_back_kernel(place_ref, *refs):
    on_core(place_ref, lambda core: attend_back_body(core, *refs))


def attend_back_body(
    core,
    q_ref,
    k_ref,
    v_ref,
    go0_ref,
    go1_ref,
    o0_ref,
    o1_ref,
    lse0_ref,
    lse1_ref,
    table_ref,
    gq_ref,
    gk_ref,
    gv_ref,
    gt_ref,
):
    heads, count, head_dim = q_ref.shape
    keys = k_ref.shape[1]
    scale = head_dim ** (-0.5)
    half_tiles = count // TILE // 2
    gt_ref[...] = jnp.zeros_like(gt_ref)
    for head in range(heads):
        key = k_ref[head]
        value = v_ref[head]
        grad_key = jnp.zeros((keys, head_dim), F32)
        grad_value = jnp.zeros((keys, head_dim), F32)
        for tile in range(count // TILE):
            go_ref, o_ref, lse_ref = (
                (go0_ref, o0_ref, lse0_ref) if tile < half_tiles else (go1_ref, o1_ref, lse1_ref)
            )
            inner = slice((tile % half_tiles) * TILE, (tile % half_tiles + 1) * TILE)
            span = slice(tile * TILE, (tile + 1) * TILE)
            starts = table_starts(core, tile, keys)
            query = q_ref[head, span, :]
            grad_out = go_ref[head, inner, :]
            scores = dot(key, query, 1, 1) * scale + bias_tile(table_ref, head, starts)
            probs = jnp.exp(scores - lse_ref[0, head : head + 1, inner])
            grad_probs = dot(value, grad_out, 1, 1)
            out = o_ref[head * head_dim : (head + 1) * head_dim, inner].astype(F32)
            row_dot = jnp.sum(out * grad_out.astype(F32).T, axis=0, keepdims=True)
            grad_scores = probs * (grad_probs - row_dot)
            for piece, row in enumerate(starts):
                for key_tile, start in enumerate(row):
                    gt_ref[head, start : start + TILE, :] += grad_scores[
                        key_tile * TILE : (key_tile + 1) * TILE,
                        piece * LANES : (piece + 1) * LANES,
                    ]
            low = grad_scores.astype(LOW)
            grad_value = grad_value + dot(probs.astype(LOW), grad_out, 1, 0)
            grad_key = grad_key + dot(low, query, 1, 0)
            gq_ref[head, span, :] = (dot(key, low, 0, 0) * scale).T.astype(LOW)
        gk_ref[head] = (grad_key * scale).astype(LOW)
        gv_ref[head] = grad_value.astype(LOW)


def attend_back(place, parts, grad_outs, attended, logs, table, heads, pair, share, at):
    _, count, head_dim = parts.shape
    groups = heads // pair
    steps = share // pair
    half = count // 2

    def head_block(first, rows=count):
        return pl.BlockSpec(
            (pair, rows, head_dim),
            lambda i, place: (first * groups + at * steps + i, 0, 0),
        )

    out_block = pl.BlockSpec((pair, count, head_dim), lambda i, place: (i, 0, 0))
    attended_block = pl.BlockSpec(
        (pair * head_dim, half), lambda i, place: (at * steps + i, 0)
    )
    log_block = pl.BlockSpec((1, pair, half), lambda i, place: (at * steps + i, 0, 0))
    table_dims = (pair,) + table.shape[1:]
    return call(
        attend_back_kernel,
        (steps,),
        [head_block(0), head_block(1), head_block(2)]
        + [head_block(0, half)] * 2
        + [attended_block] * 2
        + [log_block] * 2
        + [pl.BlockSpec(table_dims, lambda i, place: (at * steps + i, 0, 0))],
        [out_block] * 3 + [pl.BlockSpec(table_dims, lambda i, place: (i, 0, 0))],
        [shape((share, count, head_dim), LOW)] * 3 + [shape((share,) + table.shape[1:])],
        us=14.0,
    )(place, parts, parts, parts, *grad_outs, *attended, *logs, table)


def middle_kernel(
    first_tile,
    place_ref,
    own_ref,
    got_ref,
    w0_ref,
    w1_ref,
    w2_ref,
    w3_ref,
    ob_ref,
    x_ref,
    c0_ref,
    c1_ref,
    c2_ref,
    c3_ref,
    mod_ref,
    br_ref,
    mid_ref,
    h_ref,
    gb_ref,
    cot_ref,
    sum_ref,
    w_ref,
):
    step = pl.program_id(0)

    @pl.when(step == 0)
    def _():
        rows = w0_ref.shape[0]
        core = place_ref[CORE]
        for r, piece in enumerate((w0_ref, w1_ref, w2_ref, w3_ref)):
            start = pl.multiple_of(((core ^ (r % 2)) + 2 * (r // 2)) * rows, 32)
            w_ref[pl.ds(start, rows), :] = piece[...]
        sum_ref[...] = jnp.zeros_like(sum_ref)

    piece = (step + first_tile) ^ (2 * place_ref[CHIP])
    for r, ref in enumerate((c0_ref, c1_ref, c2_ref, c3_ref)):

        @pl.when(piece == r)
        def _(ref=ref):
            cot_ref[...] = ref[...]

    joined = jnp.concatenate([own_ref[...], got_ref[...]], axis=0)
    branch = dot(joined, w_ref[...], 0, 0) + ob_ref[...]
    middle = x_ref[...].astype(F32) + mod_ref[2:3] * branch
    normed, _ = norm_rows(middle)
    br_ref[...] = branch.astype(LOW)
    mid_ref[...] = middle
    h_ref[...] = (normed * (1.0 + mod_ref[4:5]) + mod_ref[3:4]).astype(LOW)
    grad = (mod_ref[5:6] * cot_ref[...].astype(F32)).astype(LOW)
    gb_ref[...] = grad
    sum_ref[...] += column_sum(grad)


def middle_part(place, own, got, weights, bias, tokens, cotangents, mod, half):
    width = tokens.shape[1]
    rows, count = own.shape
    first = half * (count // TILE)
    low, full = shape((count, width), LOW), shape((count, width))
    side = pl.BlockSpec((rows, TILE), lambda i, place: (0, i))
    return call(
        functools.partial(middle_kernel, first),
        (count // TILE,),
        [side, side]
        + [whole((width // 4, width))] * 4
        + [whole((1, width)), tiles(width, lambda i, place: i + first)]
        + [whole((TILE, width))] * 4
        + [whole(mod.shape)],
        [tiles(width)] * 5 + [whole((1, width))],
        [low, full, low, low, low, shape((1, width))],
        [pltpu.VMEM((width, width), LOW)],
        us=7.0,
    )(place, own, got, *weights, bias, tokens, *cotangents, mod)


def feed_kernel(
    place_ref,
    h_ref,
    g_ref,
    e0_ref,
    e1_ref,
    e2_ref,
    e3_ref,
    s0_ref,
    s1_ref,
    be_ref,
    act_ref,
    ge_ref,
    sum_ref,
    b2_ref,
    gh_ref,
    we_ref,
    b2_acc,
    gh_acc,
):
    step = pl.program_id(0)
    steps = pl.num_programs(0)
    gather_rows(place_ref[BLOCK], (e0_ref, e1_ref, e2_ref, e3_ref), we_ref)
    expand = we_ref[...]
    hidden, grad = h_ref[...], g_ref[...]
    shrink = jnp.where(step < steps // 2, s0_ref[...], s1_ref[...])
    inner = dot(hidden, expand, 1, 0) + be_ref[...]
    slope = math.sqrt(2.0 / math.pi)
    square = inner * inner
    bent = jnp.tanh(slope * (inner + 0.044715 * inner * square))
    act = (0.5 * inner * (1.0 + bent)).astype(LOW)
    act_ref[...] = act
    back = 0.5 * (1.0 + bent) + 0.5 * inner * (1.0 - bent * bent) * (
        slope * (1.0 + 3 * 0.044715 * square)
    )
    grad_inner = (dot(grad, shrink, 1, 1) * back).astype(LOW)
    ge_ref[...] = grad_inner
    sum_ref[...] = column_sum(grad_inner)

    @pl.when(step == 0)
    def _():
        b2_acc[...] = dot(act, shrink, 1, 0)
        gh_acc[...] = dot(grad_inner, expand, 1, 1)

    @pl.when(step > 0)
    def _():
        b2_acc[...] += dot(act, shrink, 1, 0)
        gh_acc[...] += dot(grad_inner, expand, 1, 1)

    @pl.when(step == steps - 1)
    def _():
        b2_ref[...] = b2_acc[...].astype(LOW)
        gh_ref[...] = gh_acc[...].astype(LOW)


def feed(place, hidden, grad, expands, shrinks, bias, chunk):
    count, width = hidden.shape
    rows = expands[0].shape[0]
    inner = 2 * shrinks[0].shape[0]
    steps = inner // chunk
    half = steps // 2
    skip = width // chunk
    straight = pl.BlockSpec((rows, chunk), lambda i, place: (0, i + skip))
    swapped = pl.BlockSpec((rows, chunk), lambda i, place: (0, (i + half) % steps + skip))
    columns = pl.BlockSpec((count, chunk), lambda i, place: (0, i))
    return call(
        feed_kernel,
        (steps,),
        [
            whole(hidden.shape),
            whole(grad.shape),
            straight,
            swapped,
            straight,
            swapped,
            pl.BlockSpec((chunk, width), lambda i, place: (jnp.minimum(i, half - 1), 0)),
            pl.BlockSpec((chunk, width), lambda i, place: (jnp.maximum(i - half, 0), 0)),
            pl.BlockSpec((1, chunk), lambda i, place: (0, i)),
        ],
        [
            columns,
            columns,
            pl.BlockSpec((1, chunk), lambda i, place: (0, i)),
            whole((count, width)),
            whole((count, width)),
        ],
        [
            shape((count, inner), LOW),
            shape((count, inner), LOW),
            shape((1, inner)),
            shape((count, width), LOW),
            shape((count, width), LOW),
        ],
        [pltpu.VMEM((width, chunk), LOW)] + [pltpu.VMEM((count, width), F32)] * 2,
        us=22.0,
    )(place, hidden, grad, *expands, *shrinks, bias)


def shrink_grad_kernel(place_ref, a0_ref, a1_ref, g0_ref, g1_ref, o_ref):
    total = dot(a0_ref[...], g0_ref[...], 0, 0) + dot(a1_ref[...], g1_ref[...], 0, 0)
    o_ref[...] = total.astype(LOW)


def shrink_grad(place, acts, grads, half, chunk=384):
    count, inner = acts[0].shape
    width = grads[0].shape[1]
    steps = inner // 2 // chunk
    columns = pl.BlockSpec((count, chunk), lambda i, place: (0, i + half * steps))
    return call(
        shrink_grad_kernel,
        (steps,),
        [columns] * 2 + [whole((count, width))] * 2,
        pl.BlockSpec((chunk, width), lambda i, place: (i, 0)),
        shape((inner // 2, width), LOW),
        us=5.0,
    )(place, *acts, *grads)


def expand_grad_kernel(place_ref, h0_ref, h1_ref, g0_ref, g1_ref, *refs):
    keeps, sends, acc_ref = refs[:2], refs[2:4], refs[4]
    acc_ref[...] = dot(h0_ref[...], g0_ref[...], 0, 0) + dot(h1_ref[...], g1_ref[...], 0, 0)
    rows = keeps[0].shape[0]
    for r in range(4):
        start = pl.multiple_of((place_ref[BLOCK] ^ r) * rows, 32)
        out_ref = (sends if r % 2 else keeps)[r // 2]
        out_ref[...] = acc_ref[pl.ds(start, rows), :].astype(LOW)


def expand_grad(place, hiddens, grads, chunk=384):
    count, width = hiddens[0].shape
    inner = grads[0].shape[1]
    steps = inner // chunk
    half = steps // 2
    rows = width // 4
    straight = pl.BlockSpec((rows, chunk), lambda i, place: (0, i))
    swapped = pl.BlockSpec((rows, chunk), lambda i, place: (0, (i + half) % steps))
    return call(
        expand_grad_kernel,
        (steps,),
        [whole((count, width))] * 2 + [pl.BlockSpec((count, chunk), lambda i, place: (0, i))] * 2,
        [straight] * 2 + [swapped] * 2,
        [shape((rows, inner), LOW)] * 4,
        [pltpu.VMEM((width, chunk), F32)],
        us=10.0,
    )(place, *hiddens, *grads)


def input_grad_kernel(place_ref, h_ref, gq_ref, gk_ref, gv_ref, *refs):
    step = pl.program_id(0)
    chunk = h_ref.shape[1]
    heads, _, head_dim = gq_ref.shape
    columns = 3 * heads * head_dim
    keep_ref, send_ref, joined_ref, acc_ref = refs[-4:]

    @pl.when(step == 0)
    def _():
        for side, ref in enumerate((gq_ref, gk_ref, gv_ref)):
            for head in range(heads):
                start = (side * heads + head) * head_dim
                joined_ref[:, start : start + head_dim] = ref[head]

    total = dot(h_ref[...], joined_ref[...], 0, 0)
    acc_ref[pl.ds(pl.multiple_of(step * chunk, chunk), chunk), :] = total

    @pl.when(step == pl.num_programs(0) - 1)
    def _():
        rows = keep_ref.shape[0]
        block = place_ref[BLOCK]
        for r in range(4):
            start = pl.multiple_of((block ^ r) * rows, 32)
            out_ref = send_ref if r % 2 else keep_ref
            at = (r // 2) * columns
            out_ref[:, at : at + columns] = acc_ref[pl.ds(start, rows), :].astype(LOW)

    if len(refs) > 4:
        a0_ref, a1_ref, g0_ref, g1_ref = refs[:4]

        @pl.when(step == 0)
        def _():
            out = dot(a0_ref[...], g0_ref[...], 1, 0) + dot(a1_ref[...], g1_ref[...], 1, 0)
            rows = keep_ref.shape[0]
            first, second = out[:rows].astype(LOW), out[rows:].astype(LOW)
            own = place_ref[CORE] == 0
            keep_ref[:, 2 * columns :] = jnp.where(own, first, second)
            send_ref[:, 2 * columns :] = jnp.where(own, second, first)


def input_grad(place, hidden, grads, extra=(), chunk=384):
    heads, count, head_dim = grads[0].shape
    width = hidden.shape[1]
    columns = 3 * heads * head_dim
    more = [*extra[0], *extra[1]] if extra else []
    out = (width // 4, 2 * columns + (width if extra else 0))
    return call(
        input_grad_kernel,
        (width // chunk,),
        [pl.BlockSpec((count, chunk), lambda i, place: (0, i))]
        + [whole((heads, count, head_dim))] * 3
        + [whole(one.shape) for one in more],
        [whole(out)] * 2,
        [shape(out, LOW)] * 2,
        [pltpu.VMEM((count, columns), LOW), pltpu.VMEM((width, columns), F32)],
        us=9.0 if extra else 6.0,
    )(place, hidden, *grads, *more)


def branch_back_kernel(
    head_dim,
    place_ref,
    own_ref,
    got_ref,
    mid_ref,
    cot_ref,
    br_ref,
    w0_ref,
    w1_ref,
    mod_ref,
    gm_ref,
    gb_ref,
    ga_ref,
    sum_ref,
    w_ref,
):
    @pl.when(pl.program_id(0) == 0)
    def _():
        rows = w0_ref.shape[0]
        core = place_ref[CORE]
        w_ref[pl.ds(pl.multiple_of(core * rows, 32), rows), :] = w0_ref[...]
        w_ref[pl.ds(pl.multiple_of((1 - core) * rows, 32), rows), :] = w1_ref[...]
        sum_ref[...] = jnp.zeros_like(sum_ref)

    grad_hidden = own_ref[...].astype(F32) + got_ref[...].astype(F32)
    normed, inverse = norm_rows(mid_ref[...])
    grad_middle = cot_ref[...].astype(F32) + norm_back(
        grad_hidden * (1.0 + mod_ref[4:5]), normed, inverse
    )
    gm_ref[...] = grad_middle
    grad_branch = (mod_ref[2:3] * grad_middle).astype(LOW)
    gb_ref[...] = grad_branch
    grad_att = dot(grad_branch, w_ref[...], 1, 1).astype(LOW)
    for part in range(ga_ref.shape[0]):
        ga_ref[part] = grad_att[:, part * head_dim : (part + 1) * head_dim]
    sum_ref[0:1] += column_sum(grad_hidden)
    sum_ref[1:2] += column_sum(grad_hidden * normed)
    sum_ref[2:3] += column_sum(grad_middle * br_ref[...].astype(F32))
    sum_ref[3:4] += column_sum(grad_branch)


def branch_back(place, own, got, middle, cotangent, branch, weights, mod, head_dim):
    count, width = own.shape
    rows = width // 2
    parts = rows // head_dim
    return call(
        functools.partial(branch_back_kernel, head_dim),
        (count // TILE,),
        [tiles(width)] * 5 + [whole((width // 4, width))] * 2 + [whole(mod.shape)],
        [
            tiles(width),
            tiles(width),
            pl.BlockSpec((parts, TILE, head_dim), lambda i, place: (0, i, 0)),
            whole((8, width)),
        ],
        [
            shape((count, width)),
            shape((count, width), LOW),
            shape((parts, count, head_dim), LOW),
            shape((8, width)),
        ],
        [pltpu.VMEM((rows, width), LOW)],
        us=7.0,
    )(place, own, got, middle, cotangent, branch, *weights, mod)


def project_back_kernel(groups, place_ref, *refs):
    part_refs = refs[: 3 * groups]
    w_refs = refs[3 * groups : 3 * groups + 4]
    x_ref, gh_ref, sum_ref, bias_ref, w_ref = refs[3 * groups + 4 :]

    @pl.when(pl.program_id(0) == 0)
    def _():
        gather_rows(place_ref[BLOCK], w_refs, w_ref)
        sum_ref[...] = jnp.zeros_like(sum_ref)
        bias_ref[...] = jnp.zeros_like(bias_ref)

    pieces = [ref[part] for ref in part_refs for part in range(ref.shape[0])]
    joined = jnp.concatenate(pieces, axis=1)
    grad_hidden = dot(joined, w_ref[...], 1, 1)
    gh_ref[...] = grad_hidden.astype(LOW)
    normed, _ = norm_rows(x_ref[...].astype(F32))
    sum_ref[0:1] += column_sum(grad_hidden)
    sum_ref[1:2] += column_sum(grad_hidden * normed)
    bias_ref[...] += column_sum(joined)


def project_back(place, parts, weights, tokens, far):
    width = tokens.shape[1]
    count = tokens.shape[0] // 2
    columns = weights[0].shape[1]
    pair, _, head_dim = parts[0].shape
    steps = count // TILE

    def index(i, place):
        return (place[CHIP] ^ far) * steps + i

    return call(
        functools.partial(project_back_kernel, len(parts) // 3),
        (steps,),
        [pl.BlockSpec((pair, TILE, head_dim), lambda i, place: (0, index(i, place), 0))]
        * len(parts)
        + [whole(weights[0].shape)] * 4
        + [tiles(width, index)],
        [tiles(width), whole((8, width)), whole((1, columns))],
        [
            shape((count, width), LOW),
            shape((8, width)),
            shape((1, columns)),
        ],
        [pltpu.VMEM((width, columns), LOW)],
        us=7.0,
    )(place, *parts, *weights, tokens)


def input_back_kernel(place_ref, own_ref, got_ref, x_ref, gm0_ref, gm1_ref, mod_ref, o_ref):
    grad_hidden = own_ref[...].astype(F32) + got_ref[...].astype(F32)
    normed, inverse = norm_rows(x_ref[...].astype(F32))
    grad_middle = jnp.where(place_ref[CHIP] == 0, gm0_ref[...], gm1_ref[...])
    grad = grad_middle + norm_back(grad_hidden * (1.0 + mod_ref[1:2]), normed, inverse)
    o_ref[0] = grad.astype(LOW)


def input_back(place, own, got, tokens, grad_middles, mod):
    count, width = own.shape
    steps = count // TILE
    return call(
        input_back_kernel,
        (steps,),
        [tiles(width)] * 2
        + [tiles(width, lambda i, place: place[CHIP] * steps + i)]
        + [tiles(width)] * 2
        + [whole(mod.shape)],
        pl.BlockSpec((1, TILE, width), lambda i, place: (i, 0, 0)),
        shape((steps, TILE, width), LOW),
        us=4.0,
    )(place, own, got, tokens, *grad_middles, mod)


def result_kernel(
    place_ref,
    b0_ref,
    b1_ref,
    got_ref,
    mid0_ref,
    mid1_ref,
    cot0_ref,
    cot1_ref,
    bias_ref,
    mod_ref,
    o_ref,
    sum_ref,
):
    @pl.when(pl.program_id(0) == 0)
    def _():
        sum_ref[...] = jnp.zeros_like(sum_ref)

    def own(one, two):
        return jnp.where(place_ref[CHIP] == 0, one[...].astype(F32), two[...].astype(F32))

    branch = own(b0_ref, b1_ref) + got_ref[...].astype(F32) + bias_ref[...]
    o_ref[0] = (own(mid0_ref, mid1_ref) + mod_ref[5:6] * branch).astype(LOW)
    sum_ref[0:1] += column_sum(own(cot0_ref, cot1_ref) * branch)


def result_part(place, branches, got, middles, cotangents, bias, mod):
    count, width = got.shape
    steps = count // TILE
    return call(
        result_kernel,
        (steps,),
        [tiles(width)] * 7 + [whole((1, width)), whole(mod.shape)],
        [pl.BlockSpec((1, TILE, width), lambda i, place: (i, 0, 0)), whole((8, width))],
        [shape((steps, TILE, width), LOW), shape((8, width))],
        us=4.0,
    )(place, *branches, got, *middles, *cotangents, bias, mod)


def finish_expand_kernel(place_ref, own_ref, far_ref, o_ref):
    near = (pl.program_id(0) ^ place_ref[BLOCK]) < 2
    o_ref[...] = jnp.where(near, own_ref[...].astype(F32), far_ref[...].astype(F32))


def finish_expand(place, own, far):
    rows, columns = own.shape
    width = columns // 2
    block = pl.BlockSpec((rows, width), lambda i, place: (0, (i ^ place[BLOCK]) % 2))
    return call(
        finish_expand_kernel,
        (4,),
        [block, block],
        pl.BlockSpec((rows, width), lambda i, place: (0, i)),
        shape((rows, 2 * columns)),
        us=3.0,
    )(place, own, far)


def finish_input_kernel(place_ref, *refs):
    grads, o_ref = refs[:-1], refs[-1]
    shares = len(grads)
    part_width = o_ref.shape[1] // (6 * shares)
    for chip in range(2):

        @pl.when(place_ref[CHIP] == chip)
        def _(chip=chip):
            for share, g_ref in enumerate(grads):
                for side in range(2):
                    for part in range(3):
                        start = (side * 3 + part) * part_width
                        to = ((part * 2 + (side ^ chip)) * shares + share) * part_width
                        o_ref[:, to : to + part_width] = g_ref[:, start : start + part_width].astype(F32)


def finish_input(place, grads, columns):
    rows = grads[0].shape[0]
    out = (rows, columns)
    return call(
        finish_input_kernel,
        (1,),
        [whole(grad.shape) for grad in grads],
        whole(out),
        shape(out),
        us=3.0,
    )(place, *grads)


def swap_block(value, bits):
    return lax.ppermute(value, "blk", [(i, i ^ bits) for i in range(4)])


def swap_core(value):
    return swap_block(value, 1)


def swap_chip(value):
    return swap_block(value, 2)


def ordered(mine, other, place, axis=0):
    first = jnp.where(place == 0, mine, other)
    second = jnp.where(place == 0, other, mine)
    return jnp.concatenate([first, second], axis=axis)


def add_low(one, two):
    return (one.astype(F32) + two.astype(F32)).astype(LOW)


def stages():
    count = lax.axis_size("grp")
    bits = [1 << i for i in range(count.bit_length() - 1)]
    return [bits[:1]] + [bits[i : i + 2] for i in range(1, len(bits), 2)]


def stage_place(stage):
    at = 0
    for bit in stage:
        own = lax.axis_index("blk") % 2 if bit == 0 else (lax.axis_index("grp") // bit) % 2
        at = 2 * at + own
    return at


def swap_stage(values, stage):
    groups, size = lax.axis_size("grp"), lax.axis_size("blk")
    got = [values[0]]
    for mask in range(1, 1 << len(stage)):
        chosen = [bit for i, bit in enumerate(stage) if mask >> (len(stage) - 1 - i) & 1]
        core_flip = int(0 in chosen)
        group_flip = sum(chosen)
        if group_flip and core_flip:
            pairs = [
                (g * size + i, (g ^ group_flip) * size + (i ^ 1))
                for g in range(groups)
                for i in range(size)
            ]
            got.append(lax.ppermute(values[mask], ("grp", "blk"), pairs))
        elif group_flip:
            pairs = [(g, g ^ group_flip) for g in range(groups)]
            got.append(lax.ppermute(values[mask], "grp", pairs))
        else:
            got.append(swap_core(values[mask]))
    return got


def scatter_stage(value, stage, axis):
    place = stage_place(stage)
    size = value.shape[axis] >> len(stage)
    cut = [
        lax.dynamic_slice_in_dim(value, (place ^ mask) * size, size, axis)
        for mask in range(1 << len(stage))
    ]
    return sum(one.astype(F32) for one in swap_stage(cut, stage)).astype(LOW)


def gather_stage(value, stage, axis=0):
    place = stage_place(stage)
    count = 1 << len(stage)
    got = swap_stage([value] * count, stage)
    parts = []
    for at in range(count):
        part = got[count - 1]
        for mask in range(count - 1):
            part = jnp.where(place == at ^ mask, got[mask], part)
        parts.append(part)
    return jnp.concatenate(parts, axis=axis)


def total_stage(value, stage):
    return sum(swap_stage([value] * (1 << len(stage)), stage))


class Far:
    def __init__(self, share):
        self.value = swap_chip(share)
        self.left = stages()

    @staticmethod
    def steps():
        return [[bit] for stage in stages() for bit in stage]

    @staticmethod
    def share_of(value):
        rows = value.shape[0] // lax.axis_size("grp")
        at = 0
        for stage in stages():
            at = (at << len(stage)) + stage_place(stage)
        return lax.dynamic_slice_in_dim(value, at * rows, rows, 0)

    def gather(self):
        if self.left:
            self.value = gather_stage(self.value, self.left.pop())


def after(value, *others):
    return lax.optimization_barrier((value, *others))[0]


class Sum:
    def __init__(self, keep, send, columns):
        self.value = add_low(keep, swap_core(send))
        self.columns = columns
        self.down = stages()
        self.up = []

    def step(self, *others):
        self.value = after(self.value, *others) if others else self.value
        if self.down:
            stage = self.down.pop(0)
            self.value = scatter_stage(self.value, stage, 0)
            self.up.append(stage)
            if not self.down:
                self.far = swap_chip(self.value[:, self.columns : 2 * self.columns])
        elif self.up:
            if self.far is not None:
                self.value = lax.dynamic_update_slice_in_dim(
                    self.value, self.far, self.columns, 1
                )
                self.far = None
            self.value = gather_stage(self.value, self.up.pop())
        return self.value

    def finish(self):
        while self.down or self.up:
            self.step()
        return self.value


def table_lines(table, side):
    span = 2 * side - 1
    per = LANES // side
    heads = table.shape[1]
    count = 2 * side - per
    flipped = table.T.reshape(heads, span, span)[:, ::-1]
    lines = [flipped[:, per - 1 - k : per - 1 - k + count] for k in range(per)]
    upper = jnp.concatenate([line[:, :, side - 1 :] for line in lines], axis=2)
    lower = jnp.concatenate(
        [jnp.pad(line[:, :, : side - 1], ((0, 0), (0, 0), (1, 0))) for line in lines], axis=2
    )
    return upper, lower


def table_from_lines(upper, lower, side):
    span = 2 * side - 1
    per = LANES // side
    heads, count, _ = upper.shape
    total = 0.0
    for k in range(per):
        line = jnp.concatenate(
            [lower[:, :, k * side + 1 : (k + 1) * side], upper[:, :, k * side : (k + 1) * side]],
            axis=2,
        )
        before = per - 1 - k
        total = total + jnp.pad(line, ((0, 0), (before, span - count - before), (0, 0)))
    return total[:, ::-1].reshape(heads, span * span)


def embedding(step_values, width):
    half_width = width // 2
    frequency = jnp.exp(-math.log(10000.0) * jnp.arange(half_width, dtype=F32) / half_width)
    angles = step_values.astype(F32)[:, None] * frequency[None, :]
    return jnp.concatenate([jnp.cos(angles), jnp.sin(angles)], axis=-1)


def pick(value, place, axis=0):
    return lax.dynamic_index_in_dim(value, place, axis, keepdims=False)


def shards(
    images,
    cotangent,
    timestep,
    input_weight,
    input_bias,
    output_weight,
    output_bias,
    expand_weight,
    expand_bias,
    shrink_weight,
    shrink_bias,
    modulate_weight,
    modulate_bias,
    position_table,
):
    width = images.shape[2]
    heads_all = position_table.shape[1]
    head_dim = width // heads_all
    heads = heads_all // 2
    pair = 2
    own_rows = modulate_weight.shape[0]
    block = lax.axis_index("blk").astype(jnp.int32)
    chip, core = block // 2, block % 2
    place = jnp.stack([block, chip, core])

    condition = jax.nn.silu(embedding(timestep, width)).astype(LOW)
    condition_own = lax.dynamic_slice_in_dim(condition, block * own_rows, own_rows, 1)
    partial = jnp.dot(condition_own, modulate_weight, preferred_element_type=F32)
    partial = partial.reshape(2, -1, LANES)
    partial_mine, partial_other = pick(partial, core), pick(partial, 1 - core)
    summed = (partial_mine + swap_block(partial_other, 1)) + (
        swap_block(partial_mine, 2) + swap_block(partial_other, 3)
    )
    mod = (summed.reshape(-1) + modulate_bias).reshape(6, width)

    out_share, expand_share = Far.share_of(output_weight), Far.share_of(expand_weight)
    far = Far(
        jnp.concatenate(
            [out_share]
            + [
                lax.dynamic_slice_in_dim(expand_share, (block ^ bits) * width, width, 1)
                for bits in (2, 3)
            ],
            axis=1,
        )
    )

    in_mine, in_other = pack_input(place, after(input_weight, partial_mine))
    in_far = swap_chip(in_other)

    def mine_and_other(value):
        return pick(value, core), pick(value, 1 - core)

    token_mine, token_other = mine_and_other(after(images, partial_mine))
    token_pieces = (
        token_mine,
        swap_block(token_other, 1),
        swap_block(token_mine, 2),
        swap_block(token_other, 3),
    )
    in_mine_got = swap_core(after(in_mine, token_pieces[1], summed))
    feed_mine = pack_feed(place, after(output_weight, in_mine), expand_weight)
    feed_mine_got = swap_core(after(feed_mine, in_mine_got))
    far.gather()
    weights_in = (in_mine, in_mine_got, in_far, swap_core(after(in_far, feed_mine_got)))

    def own_half(vector):
        size = vector.shape[0] // 2
        return lax.dynamic_slice_in_dim(vector, chip * size, size, 0)

    bias_in = jnp.concatenate(
        [
            own_half(input_bias[:width]),
            jnp.zeros((width // 2,), F32),
            own_half(input_bias[width:]),
        ]
    )[None]
    expand_bias_blocks = expand_bias.reshape(4, -1)
    bias_expand = jnp.concatenate(
        [pick(expand_bias_blocks, block), pick(expand_bias_blocks, block ^ 1)]
    )[None]
    upper, lower = table_lines(
        lax.dynamic_slice_in_dim(position_table, chip * heads, heads, 1), GRID
    )
    table = spread_table(place, upper, lower, GRID)

    tokens, hidden_one, parts = project(
        place,
        token_pieces,
        after(mod, feed_mine_got, table),
        weights_in,
        bias_in,
        head_dim,
    )
    cot_mine, cot_other = mine_and_other(after(cotangent, token_pieces[2], token_pieces[3]))
    cot_pieces = (
        cot_mine,
        swap_block(cot_other, 1),
        swap_block(cot_mine, 2),
        swap_block(cot_other, 3),
    )
    attended, logs = [None, None], [None, None]
    attended[0], logs[0] = attend(
        place, after(parts, cot_pieces[1], far.value), table, heads, pair, 0
    )
    far.gather()
    shrink_got = swap_core(after(shrink_weight, cot_pieces[1]))
    weights_shrink = (shrink_weight, shrink_got)
    attended_got = [swap_chip(attended[0]), None]
    attended[1], logs[1] = attend(
        place, after(parts, shrink_got, far.value, attended[0]), table, heads, pair, 1
    )
    attended_got[1] = swap_chip(attended[1])
    weights_feed = (feed_mine, feed_mine_got, far.value, swap_core(far.value))

    def forward_half(half, attended_half):
        one = middle_part(
            place,
            attended_half,
            attended_got[half],
            weights_feed,
            output_bias[None],
            tokens,
            cot_pieces,
            mod,
            half,
        )
        two = feed(
            place, one[2], one[3], weights_feed, weights_shrink, bias_expand, FEED_CHUNK
        )
        return one + two

    forward = [forward_half(0, attended[0])]
    grad_hidden_two_got = [swap_chip(forward[0][-1])]
    forward.append(forward_half(1, after(attended[1], forward[0][-1])))
    grad_hidden_two_got.append(swap_chip(forward[1][-1]))
    (
        branch_one,
        middle,
        hidden_two,
        grad_branch_two,
        cots,
        shrink_sums,
        activated,
        grad_expanded,
        expand_sums,
        branch_two,
        grad_hidden_two,
    ) = zip(*forward)

    shrink_send = shrink_grad(
        place, (after(activated[0], grad_hidden_two_got[0]), activated[1]), grad_branch_two, 1
    )
    shrink_keep = shrink_grad(place, activated, grad_branch_two, 0)
    shrink_own = add_low(shrink_keep, swap_core(shrink_send))
    expand_keep0, expand_keep1, expand_send0, expand_send1 = expand_grad(
        place, (after(hidden_two[0], shrink_keep), hidden_two[1]), grad_expanded
    )
    expand_own = add_low(expand_keep0, swap_core(expand_send0))
    expand_far = add_low(expand_keep1, swap_core(expand_send1))
    total_shrink, total_own, total_far = lax.psum((shrink_own, expand_own, expand_far), "grp")

    def branch_half(half, *others):
        return branch_back(
            place,
            grad_hidden_two[half],
            grad_hidden_two_got[half],
            after(middle[half], *others),
            cots[half],
            branch_one[half],
            weights_feed[:2],
            mod,
            head_dim,
        )

    grad_middle, grad_branch_one, grad_attended, sums_two = zip(
        branch_half(0, shrink_own), branch_half(1, expand_own, expand_far)
    )
    branch_two_send = jnp.where(chip == 0, branch_two[1], branch_two[0])

    def attend_share(at, *others):
        return attend_back(
            place,
            after(parts, *others),
            grad_attended,
            attended,
            logs,
            table,
            heads,
            pair,
            heads // SHARES,
            at,
        )

    share_columns = width * 3 // (2 * SHARES)
    share = attend_share(0)
    branch_two_got = swap_chip(after(branch_two_send, share[0]))
    keep, send = input_grad(
        place, hidden_one, share[:3], (attended, grad_branch_one), 384
    )
    input_total = Sum(keep, send, share_columns)
    grad_parts, table_grads = share[:3], share[3:]
    grad_hidden_far, sums_far, bias_far = project_back(
        place, grad_parts, weights_in, after(tokens, input_total.value), 1
    )
    input_total.step()
    first_cut = input_total.value
    grad_hidden_got = swap_chip(grad_hidden_far)
    grad_hidden_own, sums_own, bias_own = project_back(
        place, grad_parts, weights_in, after(tokens, grad_hidden_far), 0
    )
    result_half, gate_sums = result_part(
        place,
        branch_two,
        branch_two_got,
        middle,
        cots,
        shrink_bias[None],
        after(mod, grad_hidden_own, first_cut),
    )
    input_total.step()
    input_total.step()
    far_got = swap_chip(total_far)
    input_total.step(total_far)
    grad_tokens = input_back(
        place, grad_hidden_own, grad_hidden_got, tokens, grad_middle, mod
    )

    def to_blocks(value):
        return ordered(value[0][None], swap_core(value[1])[None], core)

    result = to_blocks(result_half)
    grad_images = to_blocks(grad_tokens)
    total_shrink = total_shrink.astype(F32)
    total_expand = finish_expand(place, total_own, far_got)
    totals = [input_total.finish()]
    total_input = finish_input(place, totals, 3 * width)
    total_output = totals[0][:, 2 * share_columns :].astype(F32)

    half_width = width // 2
    folded = [fold_table(place, grads, GRID) for grads in table_grads]
    table_vector = table_from_lines(
        jnp.concatenate([one for one, _ in folded]),
        jnp.concatenate([two for _, two in folded]),
        GRID,
    )
    projected_bias = (bias_far + bias_own)[0]
    expand_sum = (expand_sums[0] + expand_sums[1]).reshape(2, -1)
    split_vector = jnp.concatenate(
        [
            table_vector.reshape(-1),
            projected_bias[:half_width],
            projected_bias[2 * half_width :],
            ordered(expand_sum[0], expand_sum[1], core),
        ]
    )
    sums_two = sums_two[0] + sums_two[1]
    both_vector = jnp.concatenate([sums_two[3], (shrink_sums[0] + shrink_sums[1])[0]])
    split_rows = -(-split_vector.shape[0] // LANES)
    split_vector_padded = jnp.pad(split_vector, (0, split_rows * LANES - split_vector.shape[0]))
    small = jnp.concatenate([split_vector_padded, both_vector]).reshape(-1, LANES)
    small = after(small, first_cut)
    ends = [[0]] + Far.steps()
    for stage in ends:
        small = total_stage(small, stage)
    small_own = small[:split_rows]
    small_two = ordered(small_own[None], swap_chip(small_own)[None], chip).reshape(2, -1)
    table_size = table_vector.size
    table_total = small_two[:, :table_size].reshape(heads_all, -1).T
    at = table_size
    bias_query = small_two[:, at : at + half_width]
    bias_value = small_two[:, at + half_width : at + 2 * half_width]
    at = at + 2 * half_width
    bias_expand_total = small_two[:, at : at + expand_sum.size].reshape(-1)
    bias_input_total = jnp.stack([bias_query, bias_value]).reshape(-1)
    both = small[split_rows:].reshape(2, width)

    def own_part(vector):
        size = vector.shape[0] // 4
        return lax.dynamic_slice_in_dim(vector, block * size, size, 0)

    sums_one = sums_far + sums_own
    split_sums = jnp.stack([sums_one[0], sums_one[1], gate_sums[0]]).reshape(-1, LANES)
    split_sums = (split_sums + swap_chip(split_sums)).reshape(3, width)
    image_row = jnp.concatenate(
        [
            split_sums[0],
            split_sums[1],
            sums_two[2],
            sums_two[0],
            sums_two[1],
            split_sums[2],
            pick(condition, core).astype(F32),
        ]
    ).astype(LOW)
    rows = image_row.reshape(1, -1, LANES)
    for stage in ends:
        rows = gather_stage(rows, stage)
    rows = rows.reshape(rows.shape[0], -1)
    grads_all, conditions = rows[:, : 6 * width], rows[:, 6 * width :]
    conditions_own = lax.dynamic_slice_in_dim(conditions, block * own_rows, own_rows, 1)
    modulate_grad = dot(conditions_own, grads_all, 0, 0)
    modulate_bias_grad = own_part(jnp.sum(grads_all.astype(F32), axis=0))

    return (
        result,
        grad_images,
        total_input,
        own_part(bias_input_total),
        total_output,
        own_part(both[0]),
        total_expand,
        own_part(bias_expand_total),
        total_shrink,
        own_part(both[1]),
        modulate_grad,
        modulate_bias_grad,
        table_total,
    )


def solution(mesh):
    return jax.shard_map(
        shards,
        mesh=mesh,
        in_specs=(
            P("grp", "blk", None),
            P("grp", "blk", None),
            P("grp"),
            P("blk", None),
            P(),
            P("blk", None),
            P(),
            P("blk", None),
            P(),
            P("blk", None),
            P(),
            P("blk", None),
            P(),
            P(),
        ),
        out_specs=(
            P("grp", "blk", None),
            P("grp", "blk", None),
            P("blk", None),
            P("blk"),
            P("blk", None),
            P("blk"),
            P("blk", None),
            P("blk"),
            P("blk", None),
            P("blk"),
            P("blk", None),
            P("blk"),
            P(),
        ),
        check_vma=False,
    )
```
